128 devices in a mesh: gy: 32 (over z, y, x_lo), gz: 4 (over x_hi, core).
Axes of the slice: x: 4 (x_hi: 2, x_lo: 2; x = x_hi * 2 + x_lo), y: 4, z: 4, core: 2. Of those that a mesh axis runs over, the one named last changes fastest.
Arguments:
- estimate: float32 [128, 512, 512], P('gz', 'gy'), may hold values from 0.5 to 2
- observed: float32 [4, 128, 512, 512], P(None, 'gz', 'gy'), may hold values from 0.25 to 4
- tile_order: int32 [4, 32], replicated, may hold values from 0 to 31, each once within a row
- lateral_taps: float32 [4, 2, 9], replicated, may hold values from 0.02 to 0.2
- axial_taps: float32 [4, 33], replicated, may hold values from 0.01 to 0.06
Outputs:
- updated: float32 [128, 512, 512], P('gz', 'gy')
The draws below stay inside these ranges and needn't reach their ends.
Inputs may be any that keep to these rules, and one draw needn't show every extreme that they name: `tile_order`: each row is a permutation of the 32 tiles.
All inputs are finite; a program needn't handle non-finite values.
Results may differ from the reference program's by a relative error of at most 0.00005.
Values sent between devices are 32-bit elements; how exact they have to be, the bound alone decides.
A program may use at most 256 MiB of HBM per device.

```python
import math
import jax
import jax.numpy as jnp

Y_DEV = 16
NV = 4
TAX = 33
TLAT = 9
TILES = 32
LAT = 512
Z = 128


def block_levels(rng, dims, shards, least, high):
    level = 1.0
    for position, parts in shards:
        steps = jax.random.uniform(jax.random.fold_in(jax.random.fold_in(rng, 6), position), (parts,), jnp.float32, least / len(shards), high / len(shards))
        level = level * jnp.repeat(jnp.exp(steps), dims[position] // parts).reshape((-1,) + (1,) * (len(dims) - 1 - position))
    return level


def setup_inputs(seed: int = 0) -> dict:
    arg_keys = jax.random.split(jax.random.key(seed), 6)
    return {
        "estimate": jnp.clip(jnp.exp(math.log(2.0) - 1.3862944 * jax.random.uniform(arg_keys[0], (Z, LAT, LAT), jnp.float32) ** block_levels(arg_keys[0], (Z, LAT, LAT), ((0, 4), (1, 32)), -0.2, 0.2)), 0.5, 2.0),
        "observed": jnp.clip(jnp.exp(math.log(4.0) - 2.7725887 * jax.random.uniform(arg_keys[1], (NV, Z, LAT, LAT), jnp.float32) ** block_levels(arg_keys[1], (NV, Z, LAT, LAT), ((1, 4), (2, 32)), -0.2, 0.2)), 0.25, 4.0),
        "tile_order": jax.vmap(lambda own: jax.random.permutation(own, TILES))(jax.random.split(arg_keys[2], NV)).reshape((NV, TILES)).astype(jnp.int32),
        "lateral_taps": jnp.clip(jnp.exp(jax.random.uniform(arg_keys[3], (NV, 2, TLAT), jnp.float32, math.log(0.02), math.log(0.2))), 0.02, 0.2),
        "axial_taps": jnp.clip(jnp.exp(jax.random.uniform(arg_keys[4], (NV, TAX), jnp.float32, math.log(0.01), math.log(0.06))), 0.01, 0.06),
    }


def smear(field, plane_taps, row_taps, col_taps):
    half_planes = plane_taps.shape[0] // 2
    half_lat = row_taps.shape[0] // 2
    num_planes, num_rows, num_cols = field.shape
    padded = jnp.pad(field, ((half_planes, half_planes), (half_lat, half_lat), (half_lat, half_lat)))
    planes = plane_taps[0] * padded[0:num_planes]
    for k in range(1, plane_taps.shape[0]):
        planes = planes + plane_taps[k] * padded[k:k + num_planes]
    lined = row_taps[0] * planes[:, 0:num_rows]
    for k in range(1, row_taps.shape[0]):
        lined = lined + row_taps[k] * planes[:, k:k + num_rows]
    result = col_taps[0] * lined[:, :, 0:num_cols]
    for k in range(1, col_taps.shape[0]):
        result = result + col_taps[k] * lined[:, :, k:k + num_cols]
    return result


def reference(estimate, observed, tile_order, lateral_taps, axial_taps):
    inverse = jnp.argsort(tile_order, axis=1).astype(jnp.int32)
    summed = jnp.zeros(estimate.shape, jnp.float32)
    for view_index in range(NV):
        blurred = smear(estimate, axial_taps[view_index], lateral_taps[view_index, 0], lateral_taps[view_index, 1])
        tiled = observed[view_index].reshape(Z, TILES, Y_DEV, LAT)
        tiled = jnp.take(tiled, inverse[view_index], axis=1)
        aligned = tiled.reshape(Z, LAT, LAT).transpose(0, 2, 1)
        ratio_field = aligned / blurred
        summed = summed + smear(ratio_field, axial_taps[view_index][::-1], lateral_taps[view_index, 0][::-1], lateral_taps[view_index, 1][::-1])
    return estimate * (summed / NV)
```

```python
import functools

import jax
import jax.numpy as jnp
from jax import lax
from jax.experimental import pallas as pl
from jax.experimental.pallas import tpu as pltpu
from jax.sharding import PartitionSpec as P

MESH = pl.DeviceIdType.MESH
F32 = jnp.float32
BF16 = jnp.bfloat16

NV = 4
TAX = 33
TLAT = 9
PL = 32
RW = 16
W = 512
PEERS = 32
SLABS = 4
HZ = TAX // 2
HY = TLAT // 2
PE = PL + 2 * HZ
RE = RW + 2 * HY
ZG = PL // 8
CC = W // 128


def split(value):
    high = value.astype(BF16)
    return high, (value - high.astype(F32)).astype(BF16)


def dot(a, b):
    return jnp.dot(a, b, preferred_element_type=F32)


def dot_nt(a, b):
    return lax.dot_general(a, b, (((1,), (1,)), ((), ())), preferred_element_type=F32)


def swap_chunks(vals, chunk):
    span = vals[0].shape[-1]
    which = lax.broadcasted_iota(jnp.int32, vals[0].shape, vals[0].ndim - 1) // chunk
    for b in (4, 2, 1):
        low = (which & b) == 0
        new = list(vals)
        for k in range(8):
            if k & b:
                continue
            new[k] = jnp.where(low, vals[k], pltpu.roll(vals[k | b], b * chunk, 1))
            new[k | b] = jnp.where(low, pltpu.roll(vals[k], span - b * chunk, 1), vals[k | b])
        vals = new
    return vals


def kernel(
    est_hbm, obs_hbm, order, lat, axial, out_ref,
    est_v, obs_v, snd, rcv, ext, axb, lh, ll, bl, qh, ql, rh, rl, tt, acat, at_h, at_l, gb, zr, yr,
    lsem, a_send, a_recv, y_send, y_recv, z_send, z_recv, zb_send, zb_recv, yb_send, yb_recv,
):
    gy = lax.axis_index("gy")
    gz = lax.axis_index("gz")
    cz, cy, cx = gy // 8, (gy // 2) % 4, gy % 2

    est_in = [
        pltpu.make_async_copy(est_hbm.at[:, c * 128 : (c + 1) * 128], est_v.at[c], lsem.at[NV + c])
        for c in range(CC)
    ]
    for copy in est_in:
        copy.start()
    for v in range(NV):
        pltpu.make_async_copy(obs_hbm.at[v], obs_v.at[v], lsem.at[v]).start()

    def peer(k):
        return ((cz + k // 8) % 4) * 8 + ((cy + (k // 2) % 4) % 4) * 2 + (cx + k % 2) % 2

    bar = pltpu.get_barrier_semaphore()

    def greet(k, carry):
        pl.semaphore_signal(bar, inc=1, device_id=(peer(k), gz), device_id_type=MESH)
        return carry

    lax.fori_loop(1, PEERS, greet, 0)
    up_z, dn_z = (gz + 1) % SLABS, (gz + SLABS - 1) % SLABS
    up_y, dn_y = (gy + 1) % PEERS, (gy + PEERS - 1) % PEERS
    for other in (up_z, dn_z):
        pl.semaphore_signal(bar, inc=1, device_id=(gy, other), device_id_type=MESH)

    for c, copy in enumerate(est_in):
        copy.wait()
        for y in range(RW):
            ext[HY + y, HZ : HZ + PL, c * 128 : (c + 1) * 128] = est_v[c, pl.ds(y, PL, stride=RW), :]

    @pl.when(gy == 0)
    def _():
        ext[0:HY, HZ : HZ + PL, :] = jnp.zeros((HY, PL, W), F32)

    @pl.when(gy == PEERS - 1)
    def _():
        ext[HY + RW : RE, HZ : HZ + PL, :] = jnp.zeros((HY, PL, W), F32)

    @pl.when(gz == 0)
    def _():
        ext[:, 0:HZ, :] = jnp.zeros((RE, HZ, W), F32)

    @pl.when(gz == SLABS - 1)
    def _():
        ext[:, HZ + PL : PE, :] = jnp.zeros((RE, HZ, W), F32)

    pl.semaphore_wait(bar, PEERS - 1 + 2)

    def y_copy(side):
        src = (slice(HY, 2 * HY), slice(RW, RW + HY))[side]
        dst = (slice(HY + RW, RE), slice(0, HY))[side]
        return pltpu.make_async_remote_copy(
            ext.at[src, HZ : HZ + PL], ext.at[dst, HZ : HZ + PL], y_send.at[side], y_recv.at[side],
            device_id=((dn_y, up_y)[side], gz), device_id_type=MESH,
        )

    def z_copy(side, part):
        rows = (slice(HY, HY + RW), slice(0, HY), slice(HY + RW, RE))[part]
        src = (slice(HZ, 2 * HZ), slice(PL, PL + HZ))[side]
        dst = (slice(HZ + PL, PE), slice(0, HZ))[side]
        return pltpu.make_async_remote_copy(
            ext.at[rows, src], ext.at[rows, dst], z_send.at[side, part], z_recv.at[side, part],
            device_id=(gy, (dn_z, up_z)[side]), device_id_type=MESH,
        )

    has_y = (gy > 0, gy < PEERS - 1)
    has_z = (gz > 0, gz < SLABS - 1)
    for side in range(2):

        @pl.when(has_y[side])
        def _():
            y_copy(side).start()

        @pl.when(has_z[side])
        def _():
            z_copy(side, 0).start()

    def send_view(v, carry):
        pltpu.make_async_copy(obs_hbm.at[v], obs_v.at[v], lsem.at[v]).wait()
        for g in range(ZG):
            for c in range(4):
                t = obs_v[v, g * 128 : (g + 1) * 128, c * 128 : (c + 1) * 128].T
                for d in range(8):
                    snd[v, c * 8 + d, g] = t[d * RW : (d + 1) * RW, :]
        rcv[v, gy] = snd[v, gy]

        def push(k, inner):
            to = peer(k)
            pltpu.make_async_remote_copy(
                snd.at[v, to], rcv.at[v, gy], a_send.at[v], a_recv.at[v],
                device_id=(to, gz), device_id_type=MESH,
            ).start()
            return inner

        lax.fori_loop(1, PEERS, push, 0)
        return carry

    lax.fori_loop(0, NV, send_view, 0)

    i0 = lax.broadcasted_iota(jnp.int32, (PL, PE), 0)
    i1 = lax.broadcasted_iota(jnp.int32, (PL, PE), 1)
    for v in range(NV):
        am = jnp.zeros((PL, PE), F32)
        for k in range(TAX):
            am = jnp.where(i1 - i0 == k, axial[v, k], am)
        high, low = split(am)
        acat[v * PL : (v + 1) * PL, :] = jnp.concatenate([high, high, low], axis=1)
    lane = lax.broadcasted_iota(jnp.int32, (1, NV * PL), 1)
    j0 = lax.broadcasted_iota(jnp.int32, (PE, NV * PL), 0)
    j1 = lax.broadcasted_iota(jnp.int32, (PE, NV * PL), 1) % PL
    am = jnp.zeros((PE, NV * PL), F32)
    for k in range(TAX):
        tap = jnp.zeros((1, NV * PL), F32)
        for v in range(NV):
            tap = jnp.where(lane // PL == v, axial[v, k], tap)
        am = jnp.where(j0 - j1 == k, tap, am)
    high, low = split(am)
    at_h[...] = jnp.concatenate([high, high], axis=1)
    at_l[...] = low

    def build(v, carry):
        col = lax.broadcasted_iota(jnp.int32, (1, W), 1)
        at = col % RW
        for s in range(PEERS):
            at = jnp.where(col // RW == s, at + order[v, s] * RW, at)
        for b in range(W // 64):
            d = lax.broadcasted_iota(jnp.int32, (64, W), 0) + (b * 64 + HY) - at
            q = jnp.zeros((64, W), F32)
            for i in range(TLAT):
                q = jnp.where(d == i, lat[v, 1, i], q)
            high, low = split(q)
            qh[v, b * 64 : (b + 1) * 64, :] = high
            ql[v, b * 64 : (b + 1) * 64, :] = low
        return carry

    lax.fori_loop(0, NV, build, 0)

    for side in range(2):

        @pl.when(has_y[1 - side])
        def _():
            y_copy(side).wait_recv()

    for side in range(2):

        @pl.when(has_z[side])
        def _():
            z_copy(side, 1).start()
            z_copy(side, 2).start()

    for side in range(2):

        @pl.when(has_z[1 - side])
        def _():
            for part in range(3):
                z_copy(side, part).wait_recv()

    def axial_row(y, carry):
        high, low = split(ext[y])
        axb[y] = dot(acat[...], jnp.concatenate([high, low, high], axis=0))
        return carry

    lax.fori_loop(0, RE, axial_row, 0)

    def row_tile(t, carry):
        v = t // 2
        taps = [lat[v, 0, j] for j in range(TLAT)]
        at = pl.multiple_of(t * 16, 16)
        m = pl.multiple_of((t % 2) * 16, 16)
        for c in range(W // 128):
            cols = slice(c * 128, (c + 1) * 128)
            rows = [axb[y, pl.ds(at, 16), cols] for y in range(RE)]
            for y in range(RW):
                acc = taps[0] * rows[y]
                for j in range(1, TLAT):
                    acc = acc + taps[j] * rows[y + j]
                high, low = split(acc)
                lh[v, pl.ds(y * PL + m, 16), cols] = high
                ll[v, pl.ds(y * PL + m, 16), cols] = low
        return carry

    lax.fori_loop(0, NV * 2, row_tile, 0)

    def col_view(v, carry):
        for n in range(2):
            cols = slice(n * 256, (n + 1) * 256)
            res = dot(lh[v], qh[v, :, cols]) + dot(ll[v], qh[v, :, cols]) + dot(lh[v], ql[v, :, cols])
            bl[v, 2 * n] = res[:, :128]
            bl[v, 2 * n + 1] = res[:, 128:]
        return carry

    lax.fori_loop(0, NV, col_view, 0)

    def back_view(v, carry):
        pltpu.make_async_copy(
            rcv.at[v, pl.ds(0, PEERS - 1)], rcv.at[v, pl.ds(0, PEERS - 1)], a_recv.at[v]
        ).wait()

        def group(g, inner):
            for s in range(PEERS // 8):
                cols = slice(s * 128, (s + 1) * 128)
                vals = swap_chunks([rcv[v, s * 8 + k, g] for k in range(8)], RW)
                for z in range(8):
                    den = bl[v, s, pl.ds(g * 8 + z, RW, stride=PL), :]
                    high, low = split(vals[z] / den)
                    at = pl.multiple_of(g * 128 + z * 16, 16)
                    rh[pl.ds(at, 16), cols] = high
                    rl[pl.ds(at, 16), cols] = low
            return inner

        lax.fori_loop(0, ZG, group, 0)
        for n in range(2):
            rows = slice(n * 256, (n + 1) * 256)
            res = dot_nt(rh[...], qh[v, rows, :]) + dot_nt(rl[...], qh[v, rows, :]) + dot_nt(rh[...], ql[v, rows, :])
            bl[v, 2 * n] = res[:, :128]
            bl[v, 2 * n + 1] = res[:, 128:]
        taps = [lat[v, 0, j] for j in range(TLAT)]

        def spread(h, inner):
            for c in range(W // 128):
                cols = slice(c * 128, (c + 1) * 128)
                rows = [bl[v, c, pl.ds(h * 256 + y, 16, stride=RW), :] for y in range(RW)]
                for y in range(RE):
                    acc = None
                    for j in range(TLAT):
                        if 0 <= y - j < RW:
                            term = taps[j] * rows[y - j]
                            acc = term if acc is None else acc + term
                    high, low = split(acc)
                    at = pl.multiple_of(v * PL + h * 16, 16)
                    tt[y, pl.ds(at, 16), cols] = high
                    tt[y, pl.ds(NV * PL + at, 16), cols] = low
            return inner

        lax.fori_loop(0, 2, spread, 0)
        return carry

    lax.fori_loop(0, NV, back_view, 0)

    def axial_back(y, carry):
        gb[y] = dot(at_h[...], tt[y]) + dot(at_l[...], tt[y, 0 : NV * PL])
        return carry

    lax.fori_loop(0, RE, axial_back, 0)

    def zb_copy(side):
        src = (slice(0, HZ), slice(HZ + PL, PE))[side]
        return pltpu.make_async_remote_copy(
            gb.at[:, src], zr.at[side], zb_send.at[side], zb_recv.at[side],
            device_id=(gy, (dn_z, up_z)[side]), device_id_type=MESH,
        )

    for side in range(2):

        @pl.when(has_z[side])
        def _():
            zb_copy(side).start()

    for side in range(2):

        @pl.when(has_z[1 - side])
        def _():
            zb_copy(side).wait_recv()
            at = (slice(PL, PL + HZ), slice(HZ, 2 * HZ))[side]

            def add(y, carry):
                gb[y, at] = gb[y, at] + zr[side, y]
                return carry

            lax.fori_loop(0, RE, add, 0)

    def yb_copy(side):
        src = (slice(0, HY), slice(HY + RW, RE))[side]
        return pltpu.make_async_remote_copy(
            gb.at[src, HZ : HZ + PL], yr.at[side], yb_send.at[side], yb_recv.at[side],
            device_id=((dn_y, up_y)[side], gz), device_id_type=MESH,
        )

    for side in range(2):

        @pl.when(has_y[side])
        def _():
            yb_copy(side).start()

    for side in range(2):

        @pl.when(has_y[1 - side])
        def _():
            yb_copy(side).wait_recv()
            base = (RW, HY)[side]
            for y in range(HY):
                gb[base + y, HZ : HZ + PL] = gb[base + y, HZ : HZ + PL] + yr[side, y]

    outs = []
    for c in range(CC):
        cols = slice(c * 128, (c + 1) * 128)
        for y in range(RW):
            est_v[c, pl.ds(y, PL, stride=RW), :] = ext[HY + y, HZ : HZ + PL, cols] * (
                gb[HY + y, HZ : HZ + PL, cols] * (1.0 / NV)
            )
        outs.append(pltpu.make_async_copy(est_v.at[c], out_ref.at[:, cols], lsem.at[NV + c]))
        outs[-1].start()
    for copy in outs:
        copy.wait()

    for side in range(2):

        @pl.when(has_y[side])
        def _():
            y_copy(side).wait_send()
            yb_copy(side).wait_send()

        @pl.when(has_z[side])
        def _():
            for part in range(3):
                z_copy(side, part).wait_send()
            zb_copy(side).wait_send()

    for v in range(NV):
        pltpu.make_async_copy(
            snd.at[v, pl.ds(0, PEERS - 1)], snd.at[v, pl.ds(0, PEERS - 1)], a_send.at[v]
        ).wait()


def local(estimate, observed, tile_order, lateral_taps, axial_taps):
    rows = PL * RW
    smem = pl.BlockSpec(memory_space=pltpu.SMEM)
    hbm = pl.BlockSpec(memory_space=pl.ANY)
    dma = pltpu.SemaphoreType.DMA
    out = pl.pallas_call(
        kernel,
        out_shape=jax.ShapeDtypeStruct((rows, W), F32),
        in_specs=[hbm, hbm, smem, smem, smem],
        out_specs=hbm,
        scratch_shapes=[
            pltpu.VMEM((CC, rows, 128), F32),
            pltpu.VMEM((NV, rows, W), F32),
            pltpu.VMEM((NV, PEERS, ZG, RW, 128), F32),
            pltpu.VMEM((NV, PEERS, ZG, RW, 128), F32),
            pltpu.VMEM((RE, PE, W), F32),
            pltpu.VMEM((RE, NV * PL, W), F32),
            pltpu.VMEM((NV, rows, W), BF16),
            pltpu.VMEM((NV, rows, W), BF16),
            pltpu.VMEM((NV, CC, rows, 128), F32),
            pltpu.VMEM((NV, W, W), BF16),
            pltpu.VMEM((NV, W, W), BF16),
            pltpu.VMEM((rows, W), BF16),
            pltpu.VMEM((rows, W), BF16),
            pltpu.VMEM((RE, 2 * NV * PL, W), BF16),
            pltpu.VMEM((NV * PL, 3 * PE), BF16),
            pltpu.VMEM((PE, 2 * NV * PL), BF16),
            pltpu.VMEM((PE, NV * PL), BF16),
            pltpu.VMEM((RE, PE, W), F32),
            pltpu.VMEM((2, RE, HZ, W), F32),
            pltpu.VMEM((2, HY, PL, W), F32),
            dma((NV + CC,)),
            dma((NV,)),
            dma((NV,)),
            dma((2,)),
            dma((2,)),
            dma((2, 3)),
            dma((2, 3)),
            dma((2,)),
            dma((2,)),
            dma((2,)),
            dma((2,)),
        ],
        compiler_params=pltpu.CompilerParams(
            collective_id=0, has_side_effects=True, vmem_limit_bytes=60 << 20
        ),
    )(
        estimate.reshape(rows, W),
        observed.reshape(NV, rows, W),
        tile_order,
        lateral_taps,
        axial_taps,
    )
    return out.reshape(PL, RW, W)


def solution(mesh):
    return jax.shard_map(
        local,
        mesh=mesh,
        in_specs=(P("gz", "gy", None), P(None, "gz", "gy", None), P(), P(), P()),
        out_specs=P("gz", "gy", None),
        check_vma=False,
    )
```

```python
import functools

import jax
import jax.numpy as jnp
from jax import lax
from jax.experimental import pallas as pl
from jax.experimental.pallas import tpu as pltpu
from jax.sharding import PartitionSpec as P

MESH = pl.DeviceIdType.MESH
F32 = jnp.float32
BF16 = jnp.bfloat16

NV = 4
TAX = 33
TLAT = 9
PL = 32
RW = 16
W = 512
PEERS = 32
SLABS = 4
HZ = TAX // 2
HY = TLAT // 2
PE = PL + 2 * HZ
RE = RW + 2 * HY
ZG = PL // 8
CC = W // 128


def split(value):
    high = value.astype(BF16)
    return high, (value - high.astype(F32)).astype(BF16)


def dot(a, b):
    return jnp.dot(a, b, preferred_element_type=F32)


def dot_nt(a, b):
    return lax.dot_general(a, b, (((1,), (1,)), ((), ())), preferred_element_type=F32)


def swap_chunks(vals, chunk):
    span = vals[0].shape[-1]
    which = lax.broadcasted_iota(jnp.int32, vals[0].shape, vals[0].ndim - 1) // chunk
    for b in (4, 2, 1):
        low = (which & b) == 0
        new = list(vals)
        for k in range(8):
            if k & b:
                continue
            new[k] = jnp.where(low, vals[k], pltpu.roll(vals[k | b], b * chunk, 1))
            new[k | b] = jnp.where(low, pltpu.roll(vals[k], span - b * chunk, 1), vals[k | b])
        vals = new
    return vals


def kernel(
    est_hbm, obs_hbm, order, lat, axial, out_ref,
    est_v, obs_v, snd, rcv, ext, axb, lh, ll, bl, qh, ql, rh, rl, tt, acat, at_h, at_l, gb, zr, yr,
    lsem, a_send, a_recv, y_send, y_recv, z_send, z_recv, zb_send, zb_recv, yb_send, yb_recv,
):
    gy = lax.axis_index("gy")
    gz = lax.axis_index("gz")
    cz, cy, cx = gy // 8, (gy // 2) % 4, gy % 2

    est_in = [
        pltpu.make_async_copy(est_hbm.at[:, c * 128 : (c + 1) * 128], est_v.at[c], lsem.at[NV + c])
        for c in range(CC)
    ]
    for copy in est_in:
        copy.start()
    for v in range(NV):
        pltpu.make_async_copy(obs_hbm.at[v], obs_v.at[v], lsem.at[v]).start()

    def peer(k):
        return ((cz + k // 8) % 4) * 8 + ((cy + (k // 2) % 4) % 4) * 2 + (cx + k % 2) % 2

    bar = pltpu.get_barrier_semaphore()

    def greet(k, carry):
        pl.semaphore_signal(bar, inc=1, device_id=(peer(k), gz), device_id_type=MESH)
        return carry

    lax.fori_loop(1, PEERS, greet, 0)
    up_z, dn_z = (gz + 1) % SLABS, (gz + SLABS - 1) % SLABS
    up_y, dn_y = (gy + 1) % PEERS, (gy + PEERS - 1) % PEERS
    for other in (up_z, dn_z):
        pl.semaphore_signal(bar, inc=1, device_id=(gy, other), device_id_type=MESH)

    for c, copy in enumerate(est_in):
        copy.wait()
        for y in range(RW):
            ext[HY + y, HZ : HZ + PL, c * 128 : (c + 1) * 128] = est_v[c, pl.ds(y, PL, stride=RW), :]

    @pl.when(gy == 0)
    def _():
        ext[0:HY, HZ : HZ + PL, :] = jnp.zeros((HY, PL, W), F32)

    @pl.when(gy == PEERS - 1)
    def _():
        ext[HY + RW : RE, HZ : HZ + PL, :] = jnp.zeros((HY, PL, W), F32)

    @pl.when(gz == 0)
    def _():
        ext[:, 0:HZ, :] = jnp.zeros((RE, HZ, W), F32)

    @pl.when(gz == SLABS - 1)
    def _():
        ext[:, HZ + PL : PE, :] = jnp.zeros((RE, HZ, W), F32)

    pl.semaphore_wait(bar, PEERS - 1 + 2)

    def y_copy(side):
        src = (slice(HY, 2 * HY), slice(RW, RW + HY))[side]
        dst = (slice(HY + RW, RE), slice(0, HY))[side]
        return pltpu.make_async_remote_copy(
            ext.at[src, HZ : HZ + PL], ext.at[dst, HZ : HZ + PL], y_send.at[side], y_recv.at[side],
            device_id=((dn_y, up_y)[side], gz), device_id_type=MESH,
        )

    def z_copy(side, part):
        rows = (slice(HY, HY + RW), slice(0, HY), slice(HY + RW, RE))[part]
        src = (slice(HZ, 2 * HZ), slice(PL, PL + HZ))[side]
        dst = (slice(HZ + PL, PE), slice(0, HZ))[side]
        return pltpu.make_async_remote_copy(
            ext.at[rows, src], ext.at[rows, dst], z_send.at[side, part], z_recv.at[side, part],
            device_id=(gy, (dn_z, up_z)[side]), device_id_type=MESH,
        )

    has_y = (gy > 0, gy < PEERS - 1)
    has_z = (gz > 0, gz < SLABS - 1)
    for side in range(2):

        @pl.when(has_y[side])
        def _():
            y_copy(side).start()

        @pl.when(has_z[side])
        def _():
            z_copy(side, 0).start()

    def send_margins():
        for side in range(2):

            @pl.when(has_y[1 - side])
            def _():
                y_copy(side).wait_recv()

        for side in range(2):

            @pl.when(has_z[side])
            def _():
                z_copy(side, 1).start()
                z_copy(side, 2).start()

    def send_view(v, carry):
        pltpu.make_async_copy(obs_hbm.at[v], obs_v.at[v], lsem.at[v]).wait()
        for g in range(ZG):
            for c in range(4):
                t = obs_v[v, g * 128 : (g + 1) * 128, c * 128 : (c + 1) * 128].T
                for d in range(8):
                    snd[v, c * 8 + d, g] = t[d * RW : (d + 1) * RW, :]
        rcv[v, gy] = snd[v, gy]

        def push(k, inner):
            to = peer(k)
            pltpu.make_async_remote_copy(
                snd.at[v, to], rcv.at[v, gy], a_send.at[v], a_recv.at[v],
                device_id=(to, gz), device_id_type=MESH,
            ).start()
            return inner

        lax.fori_loop(1, PEERS, push, 0)
        return carry

    send_view(0, 0)
    send_margins()
    lax.fori_loop(1, NV, send_view, 0)

    i0 = lax.broadcasted_iota(jnp.int32, (PL, PE), 0)
    i1 = lax.broadcasted_iota(jnp.int32, (PL, PE), 1)
    for v in range(NV):
        am = jnp.zeros((PL, PE), F32)
        for k in range(TAX):
            am = jnp.where(i1 - i0 == k, axial[v, k], am)
        high, low = split(am)
        acat[v * PL : (v + 1) * PL, :] = jnp.concatenate([high, high, low], axis=1)
    lane = lax.broadcasted_iota(jnp.int32, (1, NV * PL), 1)
    j0 = lax.broadcasted_iota(jnp.int32, (PE, NV * PL), 0)
    j1 = lax.broadcasted_iota(jnp.int32, (PE, NV * PL), 1) % PL
    am = jnp.zeros((PE, NV * PL), F32)
    for k in range(TAX):
        tap = jnp.zeros((1, NV * PL), F32)
        for v in range(NV):
            tap = jnp.where(lane // PL == v, axial[v, k], tap)
        am = jnp.where(j0 - j1 == k, tap, am)
    high, low = split(am)
    at_h[...] = jnp.concatenate([high, high], axis=1)
    at_l[...] = low

    def build(v, carry):
        col = lax.broadcasted_iota(jnp.int32, (1, W), 1)
        at = col % RW
        for s in range(PEERS):
            at = jnp.where(col // RW == s, at + order[v, s] * RW, at)
        for b in range(W // 64):
            d = lax.broadcasted_iota(jnp.int32, (64, W), 0) + (b * 64 + HY) - at
            q = jnp.zeros((64, W), F32)
            for i in range(TLAT):
                q = jnp.where(d == i, lat[v, 1, i], q)
            high, low = split(q)
            qh[v, b * 64 : (b + 1) * 64, :] = high
            ql[v, b * 64 : (b + 1) * 64, :] = low
        return carry

    lax.fori_loop(0, NV, build, 0)

    for side in range(2):

        @pl.when(has_z[1 - side])
        def _():
            for part in range(3):
                z_copy(side, part).wait_recv()

    def axial_row(y, carry):
        high, low = split(ext[y])
        axb[y] = dot(acat[...], jnp.concatenate([high, low, high], axis=0))
        return carry

    lax.fori_loop(0, RE, axial_row, 0, unroll=4)

    def row_tile(t, carry):
        v = t // 2
        taps = [lat[v, 0, j] for j in range(TLAT)]
        at = pl.multiple_of(t * 16, 16)
        m = pl.multiple_of((t % 2) * 16, 16)
        for c in range(W // 128):
            cols = slice(c * 128, (c + 1) * 128)
            rows = [axb[y, pl.ds(at, 16), cols] for y in range(RE)]
            for y in range(RW):
                acc = taps[0] * rows[y]
                for j in range(1, TLAT):
                    acc = acc + taps[j] * rows[y + j]
                high, low = split(acc)
                lh[v, pl.ds(y * PL + m, 16), cols] = high
                ll[v, pl.ds(y * PL + m, 16), cols] = low
        return carry

    lax.fori_loop(0, NV * 2, row_tile, 0)

    def col_view(v, carry):
        for n in range(2):
            cols = slice(n * 256, (n + 1) * 256)
            res = dot(lh[v], qh[v, :, cols]) + dot(ll[v], qh[v, :, cols]) + dot(lh[v], ql[v, :, cols])
            bl[v, 2 * n] = res[:, :128]
            bl[v, 2 * n + 1] = res[:, 128:]
        return carry

    lax.fori_loop(0, NV, col_view, 0)

    def back_view(v, carry):
        pltpu.make_async_copy(
            rcv.at[v, pl.ds(0, PEERS - 1)], rcv.at[v, pl.ds(0, PEERS - 1)], a_recv.at[v]
        ).wait()

        def group(g, inner):
            for s in range(PEERS // 8):
                cols = slice(s * 128, (s + 1) * 128)
                vals = swap_chunks([rcv[v, s * 8 + k, g] for k in range(8)], RW)
                for z in range(8):
                    den = bl[v, s, pl.ds(g * 8 + z, RW, stride=PL), :]
                    high, low = split(vals[z] / den)
                    at = pl.multiple_of(g * 128 + z * 16, 16)
                    rh[pl.ds(at, 16), cols] = high
                    rl[pl.ds(at, 16), cols] = low
            return inner

        lax.fori_loop(0, ZG, group, 0)
        for n in range(2):
            rows = slice(n * 256, (n + 1) * 256)
            res = dot_nt(rh[...], qh[v, rows, :]) + dot_nt(rl[...], qh[v, rows, :]) + dot_nt(rh[...], ql[v, rows, :])
            bl[v, 2 * n] = res[:, :128]
            bl[v, 2 * n + 1] = res[:, 128:]
        taps = [lat[v, 0, j] for j in range(TLAT)]

        def spread(h, inner):
            for c in range(W // 128):
                cols = slice(c * 128, (c + 1) * 128)
                rows = [bl[v, c, pl.ds(h * 256 + y, 16, stride=RW), :] for y in range(RW)]
                for y in range(RE):
                    acc = None
                    for j in range(TLAT):
                        if 0 <= y - j < RW:
                            term = taps[j] * rows[y - j]
                            acc = term if acc is None else acc + term
                    high, low = split(acc)
                    at = pl.multiple_of(v * PL + h * 16, 16)
                    tt[y, pl.ds(at, 16), cols] = high
                    tt[y, pl.ds(NV * PL + at, 16), cols] = low
            return inner

        lax.fori_loop(0, 2, spread, 0)
        return carry

    lax.fori_loop(0, NV, back_view, 0)

    def axial_back(y, carry):
        gb[y] = dot(at_h[...], tt[y]) + dot(at_l[...], tt[y, 0 : NV * PL])
        return carry

    lax.fori_loop(0, RE, axial_back, 0, unroll=4)

    def zb_copy(side):
        src = (slice(0, HZ), slice(HZ + PL, PE))[side]
        return pltpu.make_async_remote_copy(
            gb.at[:, src], zr.at[side], zb_send.at[side], zb_recv.at[side],
            device_id=(gy, (dn_z, up_z)[side]), device_id_type=MESH,
        )

    for side in range(2):

        @pl.when(has_z[side])
        def _():
            zb_copy(side).start()

    for side in range(2):

        @pl.when(has_z[1 - side])
        def _():
            zb_copy(side).wait_recv()
            at = (slice(PL, PL + HZ), slice(HZ, 2 * HZ))[side]

            def add(y, carry):
                gb[y, at] = gb[y, at] + zr[side, y]
                return carry

            lax.fori_loop(0, RE, add, 0)

    def yb_copy(side):
        src = (slice(0, HY), slice(HY + RW, RE))[side]
        return pltpu.make_async_remote_copy(
            gb.at[src, HZ : HZ + PL], yr.at[side], yb_send.at[side], yb_recv.at[side],
            device_id=((dn_y, up_y)[side], gz), device_id_type=MESH,
        )

    for side in range(2):

        @pl.when(has_y[side])
        def _():
            yb_copy(side).start()

    for side in range(2):

        @pl.when(has_y[1 - side])
        def _():
            yb_copy(side).wait_recv()
            base = (RW, HY)[side]
            for y in range(HY):
                gb[base + y, HZ : HZ + PL] = gb[base + y, HZ : HZ + PL] + yr[side, y]

    outs = []
    for c in range(CC):
        cols = slice(c * 128, (c + 1) * 128)
        for y in range(RW):
            est_v[c, pl.ds(y, PL, stride=RW), :] = ext[HY + y, HZ : HZ + PL, cols] * (
                gb[HY + y, HZ : HZ + PL, cols] * (1.0 / NV)
            )
        outs.append(pltpu.make_async_copy(est_v.at[c], out_ref.at[:, cols], lsem.at[NV + c]))
        outs[-1].start()
    for copy in outs:
        copy.wait()

    for side in range(2):

        @pl.when(has_y[side])
        def _():
            y_copy(side).wait_send()
            yb_copy(side).wait_send()

        @pl.when(has_z[side])
        def _():
            for part in range(3):
                z_copy(side, part).wait_send()
            zb_copy(side).wait_send()

    for v in range(NV):
        pltpu.make_async_copy(
            snd.at[v, pl.ds(0, PEERS - 1)], snd.at[v, pl.ds(0, PEERS - 1)], a_send.at[v]
        ).wait()


def local(estimate, observed, tile_order, lateral_taps, axial_taps):
    rows = PL * RW
    smem = pl.BlockSpec(memory_space=pltpu.SMEM)
    hbm = pl.BlockSpec(memory_space=pl.ANY)
    dma = pltpu.SemaphoreType.DMA
    out = pl.pallas_call(
        kernel,
        out_shape=jax.ShapeDtypeStruct((rows, W), F32),
        in_specs=[hbm, hbm, smem, smem, smem],
        out_specs=hbm,
        scratch_shapes=[
            pltpu.VMEM((CC, rows, 128), F32),
            pltpu.VMEM((NV, rows, W), F32),
            pltpu.VMEM((NV, PEERS, ZG, RW, 128), F32),
            pltpu.VMEM((NV, PEERS, ZG, RW, 128), F32),
            pltpu.VMEM((RE, PE, W), F32),
            pltpu.VMEM((RE, NV * PL, W), F32),
            pltpu.VMEM((NV, rows, W), BF16),
            pltpu.VMEM((NV, rows, W), BF16),
            pltpu.VMEM((NV, CC, rows, 128), F32),
            pltpu.VMEM((NV, W, W), BF16),
            pltpu.VMEM((NV, W, W), BF16),
            pltpu.VMEM((rows, W), BF16),
            pltpu.VMEM((rows, W), BF16),
            pltpu.VMEM((RE, 2 * NV * PL, W), BF16),
            pltpu.VMEM((NV * PL, 3 * PE), BF16),
            pltpu.VMEM((PE, 2 * NV * PL), BF16),
            pltpu.VMEM((PE, NV * PL), BF16),
            pltpu.VMEM((RE, PE, W), F32),
            pltpu.VMEM((2, RE, HZ, W), F32),
            pltpu.VMEM((2, HY, PL, W), F32),
            dma((NV + CC,)),
            dma((NV,)),
            dma((NV,)),
            dma((2,)),
            dma((2,)),
            dma((2, 3)),
            dma((2, 3)),
            dma((2,)),
            dma((2,)),
            dma((2,)),
            dma((2,)),
        ],
        compiler_params=pltpu.CompilerParams(
            collective_id=0, has_side_effects=True, vmem_limit_bytes=60 << 20
        ),
    )(
        estimate.reshape(rows, W),
        observed.reshape(NV, rows, W),
        tile_order,
        lateral_taps,
        axial_taps,
    )
    return out.reshape(PL, RW, W)


def solution(mesh):
    return jax.shard_map(
        local,
        mesh=mesh,
        in_specs=(P("gz", "gy", None), P(None, "gz", "gy", None), P(), P(), P()),
        out_specs=P("gz", "gy", None),
        check_vma=False,
    )
```

```python
import functools

import jax
import jax.numpy as jnp
from jax import lax
from jax.experimental import pallas as pl
from jax.experimental.pallas import tpu as pltpu
from jax.sharding import PartitionSpec as P

MESH = pl.DeviceIdType.MESH
F32 = jnp.float32
BF16 = jnp.bfloat16

NV = 4
TAX = 33
TLAT = 9
PL = 32
RW = 16
W = 512
PEERS = 32
SLABS = 4
HZ = TAX // 2
HY = TLAT // 2
PE = PL + 2 * HZ
RE = RW + 2 * HY
ZG = PL // 8
CC = W // 128


PLANE = (
    (1, 0), (0, 1), (3, 0), (0, 3), (2, 1), (1, 2), (2, 3), (3, 2), (1, 1), (3, 3), (1, 3), (3, 1), (2, 0), (0, 2), (2, 2),
)
ORDER = ((0, 0, 1),) + tuple((dz, dy, dx) for dz, dy in PLANE for dx in (1, 0))


def split(value):
    high = value.astype(BF16)
    return high, (value - high.astype(F32)).astype(BF16)


def dot(a, b):
    return jnp.dot(a, b, preferred_element_type=F32)


def dot_nt(a, b):
    return lax.dot_general(a, b, (((1,), (1,)), ((), ())), preferred_element_type=F32)


def swap_chunks(vals, chunk):
    span = vals[0].shape[-1]
    which = lax.broadcasted_iota(jnp.int32, vals[0].shape, vals[0].ndim - 1) // chunk
    for b in (4, 2, 1):
        low = (which & b) == 0
        new = list(vals)
        for k in range(8):
            if k & b:
                continue
            new[k] = jnp.where(low, vals[k], pltpu.roll(vals[k | b], b * chunk, 1))
            new[k | b] = jnp.where(low, pltpu.roll(vals[k], span - b * chunk, 1), vals[k | b])
        vals = new
    return vals


def kernel(
    est_hbm, obs_hbm, order, lat, axial, out_ref,
    est_v, obs_v, snd, rcv, ext, axb, lh, ll, bl, qh, ql, rh, rl, tt, acat, adj, gb, zr, yr,
    lsem, a_send, a_recv, y_send, y_recv, z_send, z_recv, zb_send, zb_recv, yb_send, yb_recv,
):
    gy = lax.axis_index("gy")
    gz = lax.axis_index("gz")
    cz, cy, cx = gy // 8, (gy // 2) % 4, gy % 2

    est_in = [
        pltpu.make_async_copy(est_hbm.at[:, c * 128 : (c + 1) * 128], est_v.at[c], lsem.at[NV + c])
        for c in range(CC)
    ]
    for copy in est_in:
        copy.start()
    for v in range(NV):
        pltpu.make_async_copy(obs_hbm.at[v], obs_v.at[v], lsem.at[v]).start()

    def peer(dz, dy, dx):
        return ((cz + dz) % 4) * 8 + ((cy + dy) % 4) * 2 + (cx + dx) % 2

    bar = pltpu.get_barrier_semaphore()

    for offset in ORDER:
        pl.semaphore_signal(bar, inc=1, device_id=(peer(*offset), gz), device_id_type=MESH)
    up_z, dn_z = (gz + 1) % SLABS, (gz + SLABS - 1) % SLABS
    up_y, dn_y = (gy + 1) % PEERS, (gy + PEERS - 1) % PEERS
    for other in (up_z, dn_z):
        pl.semaphore_signal(bar, inc=1, device_id=(gy, other), device_id_type=MESH)

    for c, copy in enumerate(est_in):
        copy.wait()
        for y in range(RW):
            ext[HY + y, HZ : HZ + PL, c * 128 : (c + 1) * 128] = est_v[c, pl.ds(y, PL, stride=RW), :]

    @pl.when(gy == 0)
    def _():
        ext[0:HY, HZ : HZ + PL, :] = jnp.zeros((HY, PL, W), F32)

    @pl.when(gy == PEERS - 1)
    def _():
        ext[HY + RW : RE, HZ : HZ + PL, :] = jnp.zeros((HY, PL, W), F32)

    @pl.when(gz == 0)
    def _():
        ext[:, 0:HZ, :] = jnp.zeros((RE, HZ, W), F32)

    @pl.when(gz == SLABS - 1)
    def _():
        ext[:, HZ + PL : PE, :] = jnp.zeros((RE, HZ, W), F32)

    pl.semaphore_wait(bar, PEERS - 1 + 2)

    def y_copy(side):
        src = (slice(HY, 2 * HY), slice(RW, RW + HY))[side]
        dst = (slice(HY + RW, RE), slice(0, HY))[side]
        return pltpu.make_async_remote_copy(
            ext.at[src, HZ : HZ + PL], ext.at[dst, HZ : HZ + PL], y_send.at[side], y_recv.at[side],
            device_id=((dn_y, up_y)[side], gz), device_id_type=MESH,
        )

    def z_copy(side, part):
        rows = (slice(HY, HY + RW), slice(0, HY), slice(HY + RW, RE))[part]
        src = (slice(HZ, 2 * HZ), slice(PL, PL + HZ))[side]
        dst = (slice(HZ + PL, PE), slice(0, HZ))[side]
        return pltpu.make_async_remote_copy(
            ext.at[rows, src], ext.at[rows, dst], z_send.at[side, part], z_recv.at[side, part],
            device_id=(gy, (dn_z, up_z)[side]), device_id_type=MESH,
        )

    has_y = (gy > 0, gy < PEERS - 1)
    has_z = (gz > 0, gz < SLABS - 1)
    for side in range(2):

        @pl.when(has_y[side])
        def _():
            y_copy(side).start()

        @pl.when(has_z[side])
        def _():
            z_copy(side, 0).start()

    def send_margins():
        for side in range(2):

            @pl.when(has_y[1 - side])
            def _():
                y_copy(side).wait_recv()

        for side in range(2):

            @pl.when(has_z[side])
            def _():
                z_copy(side, 1).start()
                z_copy(side, 2).start()

    def send_view(v, carry):
        pltpu.make_async_copy(obs_hbm.at[v], obs_v.at[v], lsem.at[v]).wait()
        for g in range(ZG):
            for c in range(4):
                t = obs_v[v, g * 128 : (g + 1) * 128, c * 128 : (c + 1) * 128].T
                for d in range(8):
                    snd[v, c * 8 + d, g] = t[d * RW : (d + 1) * RW, :]
        rcv[v, gy] = snd[v, gy]

        for offset in ORDER:
            to = peer(*offset)
            pltpu.make_async_remote_copy(
                snd.at[v, to], rcv.at[v, gy], a_send.at[v], a_recv.at[v],
                device_id=(to, gz), device_id_type=MESH,
            ).start()
        return carry

    send_view(0, 0)
    send_margins()
    lax.fori_loop(1, NV, send_view, 0)

    i0 = lax.broadcasted_iota(jnp.int32, (PL, PE), 0)
    i1 = lax.broadcasted_iota(jnp.int32, (PL, PE), 1)
    for v in range(NV):
        am = jnp.zeros((PL, PE), F32)
        for k in range(TAX):
            am = jnp.where(i1 - i0 == k, axial[v, k], am)
        high, low = split(am)
        acat[v * PL : (v + 1) * PL, :] = jnp.concatenate([high, high, low], axis=1)
    j0 = lax.broadcasted_iota(jnp.int32, (PE, PL), 0)
    j1 = lax.broadcasted_iota(jnp.int32, (PE, PL), 1)
    for v in range(NV):
        am = jnp.zeros((PE, PL), F32)
        for k in range(TAX):
            am = jnp.where(j0 - j1 == k, axial[v, k], am)
        high, low = split(am)
        adj[v] = jnp.concatenate([high, high, low], axis=1)

    def build(v, carry):
        col = lax.broadcasted_iota(jnp.int32, (1, W), 1)
        at = col % RW
        for s in range(PEERS):
            at = jnp.where(col // RW == s, at + order[v, s] * RW, at)
        for b in range(W // 64):
            d = lax.broadcasted_iota(jnp.int32, (64, W), 0) + (b * 64 + HY) - at
            q = jnp.zeros((64, W), F32)
            for i in range(TLAT):
                q = jnp.where(d == i, lat[v, 1, i], q)
            high, low = split(q)
            qh[v, b * 64 : (b + 1) * 64, :] = high
            ql[v, b * 64 : (b + 1) * 64, :] = low
        return carry

    lax.fori_loop(0, NV, build, 0)

    for side in range(2):

        @pl.when(has_z[1 - side])
        def _():
            for part in range(3):
                z_copy(side, part).wait_recv()

    def axial_row(y, carry):
        high, low = split(ext[y])
        axb[y] = dot(acat[...], jnp.concatenate([high, low, high], axis=0))
        return carry

    lax.fori_loop(0, RE, axial_row, 0, unroll=4)

    def row_tile(t, carry):
        v = t // 2
        taps = [lat[v, 0, j] for j in range(TLAT)]
        at = pl.multiple_of(t * 16, 16)
        m = pl.multiple_of((t % 2) * 16, 16)
        for c in range(W // 128):
            cols = slice(c * 128, (c + 1) * 128)
            rows = [axb[y, pl.ds(at, 16), cols] for y in range(RE)]
            for y in range(RW):
                acc = taps[0] * rows[y]
                for j in range(1, TLAT):
                    acc = acc + taps[j] * rows[y + j]
                high, low = split(acc)
                lh[v, pl.ds(y * PL + m, 16), cols] = high
                ll[v, pl.ds(y * PL + m, 16), cols] = low
        return carry

    lax.fori_loop(0, NV * 2, row_tile, 0)

    def col_view(v, carry):
        for n in range(2):
            cols = slice(n * 256, (n + 1) * 256)
            res = dot(lh[v], qh[v, :, cols]) + dot(ll[v], qh[v, :, cols]) + dot(lh[v], ql[v, :, cols])
            bl[v, 2 * n] = res[:, :128]
            bl[v, 2 * n + 1] = res[:, 128:]
        return carry

    lax.fori_loop(0, NV, col_view, 0)

    def back_view(v):
        pltpu.make_async_copy(
            rcv.at[v, pl.ds(0, PEERS - 1)], rcv.at[v, pl.ds(0, PEERS - 1)], a_recv.at[v]
        ).wait()

        def group(g, inner):
            for s in range(PEERS // 8):
                cols = slice(s * 128, (s + 1) * 128)
                vals = swap_chunks([rcv[v, s * 8 + k, g] for k in range(8)], RW)
                for z in range(8):
                    den = bl[v, s, pl.ds(g * 8 + z, RW, stride=PL), :]
                    high, low = split(vals[z] / den)
                    at = pl.multiple_of(g * 128 + z * 16, 16)
                    rh[pl.ds(at, 16), cols] = high
                    rl[pl.ds(at, 16), cols] = low
            return inner

        lax.fori_loop(0, ZG, group, 0)
        for n in range(2):
            rows = slice(n * 256, (n + 1) * 256)
            res = dot_nt(rh[...], qh[v, rows, :]) + dot_nt(rl[...], qh[v, rows, :]) + dot_nt(rh[...], ql[v, rows, :])
            bl[v, 2 * n] = res[:, :128]
            bl[v, 2 * n + 1] = res[:, 128:]
        taps = [lat[v, 0, j] for j in range(TLAT)]

        def spread(h, inner):
            for c in range(W // 128):
                cols = slice(c * 128, (c + 1) * 128)
                rows = [bl[v, c, pl.ds(h * 256 + y, 16, stride=RW), :] for y in range(RW)]
                for y in range(RE):
                    acc = None
                    for j in range(TLAT):
                        if 0 <= y - j < RW:
                            term = taps[j] * rows[y - j]
                            acc = term if acc is None else acc + term
                    high, low = split(acc)
                    at = pl.multiple_of(h * 16, 16)
                    tt[y, pl.ds(at, 16), cols] = high
                    tt[y, pl.ds(PL + at, 16), cols] = low
                    tt[y, pl.ds(2 * PL + at, 16), cols] = high
            return inner

        lax.fori_loop(0, 2, spread, 0)

    def axial_back(v, first, start, stop):
        def row(y, carry):
            term = dot(adj[v], tt[y])
            gb[y] = term if first else gb[y] + term
            return carry

        lax.fori_loop(start, stop, row, 0, unroll=4)

    def whole_view(v, carry):
        back_view(v)
        axial_back(v, False, 0, RE)
        return carry

    back_view(0)
    axial_back(0, True, 0, RE)
    lax.fori_loop(1, NV - 1, whole_view, 0)
    back_view(NV - 1)

    parts = ((0, HY), (HY + RW, RE), (HY, HY + RW))

    def zb_copy(side, part):
        src = (slice(0, HZ), slice(HZ + PL, PE))[side]
        rows = slice(*parts[part])
        return pltpu.make_async_remote_copy(
            gb.at[rows, src], zr.at[side, rows], zb_send.at[side, part], zb_recv.at[side, part],
            device_id=(gy, (dn_z, up_z)[side]), device_id_type=MESH,
        )

    def zb_start(part):
        for side in range(2):

            @pl.when(has_z[side])
            def _():
                zb_copy(side, part).start()

    def zb_add(part):
        for side in range(2):

            @pl.when(has_z[1 - side])
            def _():
                zb_copy(side, part).wait_recv()
                at = (slice(PL, PL + HZ), slice(HZ, 2 * HZ))[side]
                for y in range(*parts[part]):
                    gb[y, at] = gb[y, at] + zr[side, y]

    for part in range(2):
        axial_back(NV - 1, False, *parts[part])
        zb_start(part)
    axial_back(NV - 1, False, *parts[2])
    zb_start(2)
    for part in range(2):
        zb_add(part)

    def yb_copy(side):
        src = (slice(0, HY), slice(HY + RW, RE))[side]
        return pltpu.make_async_remote_copy(
            gb.at[src, HZ : HZ + PL], yr.at[side], yb_send.at[side], yb_recv.at[side],
            device_id=((dn_y, up_y)[side], gz), device_id_type=MESH,
        )

    for side in range(2):

        @pl.when(has_y[side])
        def _():
            yb_copy(side).start()

    zb_add(2)

    def finish(rows):
        for c in range(CC):
            cols = slice(c * 128, (c + 1) * 128)
            for y in rows:
                est_v[c, pl.ds(y, PL, stride=RW), :] = ext[HY + y, HZ : HZ + PL, cols] * (
                    gb[HY + y, HZ : HZ + PL, cols] * (1.0 / NV)
                )

    finish(range(HY, RW - HY))
    for side in range(2):

        @pl.when(has_y[1 - side])
        def _():
            yb_copy(side).wait_recv()
            base = (RW, HY)[side]
            for y in range(HY):
                gb[base + y, HZ : HZ + PL] = gb[base + y, HZ : HZ + PL] + yr[side, y]

    finish([*range(HY), *range(RW - HY, RW)])
    outs = []
    for c in range(CC):
        cols = slice(c * 128, (c + 1) * 128)
        outs.append(pltpu.make_async_copy(est_v.at[c], out_ref.at[:, cols], lsem.at[NV + c]))
        outs[-1].start()
    for copy in outs:
        copy.wait()

    for side in range(2):

        @pl.when(has_y[side])
        def _():
            y_copy(side).wait_send()
            yb_copy(side).wait_send()

        @pl.when(has_z[side])
        def _():
            for part in range(3):
                z_copy(side, part).wait_send()
                zb_copy(side, part).wait_send()

    for v in range(NV):
        pltpu.make_async_copy(
            snd.at[v, pl.ds(0, PEERS - 1)], snd.at[v, pl.ds(0, PEERS - 1)], a_send.at[v]
        ).wait()


def local(estimate, observed, tile_order, lateral_taps, axial_taps):
    rows = PL * RW
    smem = pl.BlockSpec(memory_space=pltpu.SMEM)
    hbm = pl.BlockSpec(memory_space=pl.ANY)
    dma = pltpu.SemaphoreType.DMA
    out = pl.pallas_call(
        kernel,
        out_shape=jax.ShapeDtypeStruct((rows, W), F32),
        in_specs=[hbm, hbm, smem, smem, smem],
        out_specs=hbm,
        scratch_shapes=[
            pltpu.VMEM((CC, rows, 128), F32),
            pltpu.VMEM((NV, rows, W), F32),
            pltpu.VMEM((NV, PEERS, ZG, RW, 128), F32),
            pltpu.VMEM((NV, PEERS, ZG, RW, 128), F32),
            pltpu.VMEM((RE, PE, W), F32),
            pltpu.VMEM((RE, NV * PL, W), F32),
            pltpu.VMEM((NV, rows, W), BF16),
            pltpu.VMEM((NV, rows, W), BF16),
            pltpu.VMEM((NV, CC, rows, 128), F32),
            pltpu.VMEM((NV, W, W), BF16),
            pltpu.VMEM((NV, W, W), BF16),
            pltpu.VMEM((rows, W), BF16),
            pltpu.VMEM((rows, W), BF16),
            pltpu.VMEM((RE, 3 * PL, W), BF16),
            pltpu.VMEM((NV * PL, 3 * PE), BF16),
            pltpu.VMEM((NV, PE, 3 * PL), BF16),
            pltpu.VMEM((RE, PE, W), F32),
            pltpu.VMEM((2, RE, HZ, W), F32),
            pltpu.VMEM((2, HY, PL, W), F32),
            dma((NV + CC,)),
            dma((NV,)),
            dma((NV,)),
            dma((2,)),
            dma((2,)),
            dma((2, 3)),
            dma((2, 3)),
            dma((2, 3)),
            dma((2, 3)),
            dma((2,)),
            dma((2,)),
        ],
        compiler_params=pltpu.CompilerParams(
            collective_id=0, has_side_effects=True, vmem_limit_bytes=60 << 20
        ),
    )(
        estimate.reshape(rows, W),
        observed.reshape(NV, rows, W),
        tile_order,
        lateral_taps,
        axial_taps,
    )
    return out.reshape(PL, RW, W)


def solution(mesh):
    return jax.shard_map(
        local,
        mesh=mesh,
        in_specs=(P("gz", "gy", None), P(None, "gz", "gy", None), P(), P(), P()),
        out_specs=P("gz", "gy", None),
        check_vma=False,
    )
```

```python
import functools

import jax
import jax.numpy as jnp
from jax import lax
from jax.experimental import pallas as pl
from jax.experimental.pallas import tpu as pltpu
from jax.sharding import PartitionSpec as P

MESH = pl.DeviceIdType.MESH
F32 = jnp.float32
BF16 = jnp.bfloat16

NV = 4
TAX = 33
TLAT = 9
PL = 32
RW = 16
W = 512
PEERS = 32
SLABS = 4
HZ = TAX // 2
HY = TLAT // 2
PE = PL + 2 * HZ
RE = RW + 2 * HY
ZG = PL // 8
CC = W // 128


PLANE = (
    (1, 0), (0, 1), (3, 0), (0, 3), (2, 1), (1, 2), (2, 3), (3, 2), (1, 1), (3, 3), (1, 3), (3, 1), (2, 0), (0, 2), (2, 2),
)
ORDER = ((0, 0, 1),) + tuple((dz, dy, dx) for dz, dy in PLANE for dx in (1, 0))


def split(value):
    high = value.astype(BF16)
    return high, (value - high.astype(F32)).astype(BF16)


def dot(a, b):
    return jnp.dot(a, b, preferred_element_type=F32)


def dot_nt(a, b):
    return lax.dot_general(a, b, (((1,), (1,)), ((), ())), preferred_element_type=F32)


def swap_chunks(vals, chunk):
    span = vals[0].shape[-1]
    which = lax.broadcasted_iota(jnp.int32, vals[0].shape, vals[0].ndim - 1) // chunk
    for b in (4, 2, 1):
        low = (which & b) == 0
        new = list(vals)
        for k in range(8):
            if k & b:
                continue
            new[k] = jnp.where(low, vals[k], pltpu.roll(vals[k | b], b * chunk, 1))
            new[k | b] = jnp.where(low, pltpu.roll(vals[k], span - b * chunk, 1), vals[k | b])
        vals = new
    return vals


def kernel(
    est_hbm, obs_hbm, order, lat, axial, out_ref,
    est_v, obs_v, snd, rcv, ext, axb, lh, ll, bl, qh, ql, rh, rl, tt, acat, adj, gb, zr, yr, dr,
    lsem, a_send, a_recv, y_send, y_recv, z_send, z_recv, zb_send, zb_recv, yb_send, yb_recv,
    d_send, d_recv, db_send, db_recv,
):
    gy = lax.axis_index("gy")
    gz = lax.axis_index("gz")
    cz, cy, cx = gy // 8, (gy // 2) % 4, gy % 2

    est_in = [
        pltpu.make_async_copy(est_hbm.at[:, c * 128 : (c + 1) * 128], est_v.at[c], lsem.at[NV + c])
        for c in range(CC)
    ]
    for copy in est_in:
        copy.start()
    for v in range(NV):
        pltpu.make_async_copy(obs_hbm.at[v], obs_v.at[v], lsem.at[v]).start()

    def peer(dz, dy, dx):
        return ((cz + dz) % 4) * 8 + ((cy + dy) % 4) * 2 + (cx + dx) % 2

    bar = pltpu.get_barrier_semaphore()

    for offset in ORDER:
        pl.semaphore_signal(bar, inc=1, device_id=(peer(*offset), gz), device_id_type=MESH)
    up_z, dn_z = (gz + 1) % SLABS, (gz + SLABS - 1) % SLABS
    up_y, dn_y = (gy + 1) % PEERS, (gy + PEERS - 1) % PEERS
    for other in (up_z, dn_z):
        pl.semaphore_signal(bar, inc=1, device_id=(gy, other), device_id_type=MESH)

    middle = gz * (SLABS - 1 - gz) // 2

    @pl.when(middle == 1)
    def _():
        for other in (up_y, dn_y):
            pl.semaphore_signal(
                bar, inc=1, device_id=(other, SLABS - 1 - gz), device_id_type=MESH
            )

    for c, copy in enumerate(est_in):
        copy.wait()
        for y in range(RW):
            ext[HY + y, HZ : HZ + PL, c * 128 : (c + 1) * 128] = est_v[c, pl.ds(y, PL, stride=RW), :]

    @pl.when(gy == 0)
    def _():
        ext[0:HY, HZ : HZ + PL, :] = jnp.zeros((HY, PL, W), F32)

    @pl.when(gy == PEERS - 1)
    def _():
        ext[HY + RW : RE, HZ : HZ + PL, :] = jnp.zeros((HY, PL, W), F32)

    @pl.when(gz == 0)
    def _():
        ext[:, 0:HZ, :] = jnp.zeros((RE, HZ, W), F32)

    @pl.when(gz == SLABS - 1)
    def _():
        ext[:, HZ + PL : PE, :] = jnp.zeros((RE, HZ, W), F32)

    for z_edge, planes in ((1, slice(HZ + PL, PE)), (2, slice(0, HZ))):
        for y_edge, rows in ((0, slice(0, HY)), (PEERS - 1, slice(HY + RW, RE))):

            @pl.when((gz == z_edge) & (gy == y_edge))
            def _():
                ext[rows, planes, :] = jnp.zeros((HY, HZ, W), F32)

    pl.semaphore_wait(bar, PEERS - 1 + 2 + 2 * middle)

    def y_copy(side):
        src = (slice(HY, 2 * HY), slice(RW, RW + HY))[side]
        dst = (slice(HY + RW, RE), slice(0, HY))[side]
        return pltpu.make_async_remote_copy(
            ext.at[src, HZ : HZ + PL], ext.at[dst, HZ : HZ + PL], y_send.at[side], y_recv.at[side],
            device_id=((dn_y, up_y)[side], gz), device_id_type=MESH,
        )

    def z_copy(side, part):
        rows = (slice(HY, HY + RW), slice(0, HY), slice(HY + RW, RE))[part]
        src = (slice(HZ, 2 * HZ), slice(PL, PL + HZ))[side]
        dst = (slice(HZ + PL, PE), slice(0, HZ))[side]
        return pltpu.make_async_remote_copy(
            ext.at[rows, src], ext.at[rows, dst], z_send.at[side, part], z_recv.at[side, part],
            device_id=(gy, (dn_z, up_z)[side]), device_id_type=MESH,
        )

    def d_copy(zs, ys):
        rows = (slice(HY, 2 * HY), slice(RW, RW + HY))[ys]
        to_rows = (slice(HY + RW, RE), slice(0, HY))[ys]
        src = (slice(HZ, 2 * HZ), slice(PL, PL + HZ))[zs]
        dst = (slice(HZ + PL, PE), slice(0, HZ))[zs]
        return pltpu.make_async_remote_copy(
            ext.at[rows, src], ext.at[to_rows, dst], d_send.at[zs, ys], d_recv.at[zs, ys],
            device_id=((dn_y, up_y)[ys], (dn_z, up_z)[zs]), device_id_type=MESH,
        )

    on_chip = (gz % 2 == 1, gz % 2 == 0)
    across = (gz == 2, gz == 1)
    has_y = (gy > 0, gy < PEERS - 1)
    has_z = (gz > 0, gz < SLABS - 1)
    for side in range(2):

        @pl.when(has_y[side])
        def _():
            y_copy(side).start()

        @pl.when(has_z[side])
        def _():
            z_copy(side, 0).start()

    for zs in range(2):
        for ys in range(2):

            @pl.when(across[zs] & has_y[ys])
            def _():
                d_copy(zs, ys).start()

    def send_margins():
        for side in range(2):

            @pl.when(has_y[1 - side])
            def _():
                y_copy(side).wait_recv()

        for side in range(2):

            @pl.when(on_chip[side])
            def _():
                z_copy(side, 1).start()
                z_copy(side, 2).start()

    def send_view(v, carry):
        pltpu.make_async_copy(obs_hbm.at[v], obs_v.at[v], lsem.at[v]).wait()
        for g in range(ZG):
            for c in range(4):
                t = obs_v[v, g * 128 : (g + 1) * 128, c * 128 : (c + 1) * 128].T
                for d in range(8):
                    snd[v, c * 8 + d, g] = t[d * RW : (d + 1) * RW, :]
        rcv[v, gy] = snd[v, gy]

        for offset in ORDER:
            to = peer(*offset)
            pltpu.make_async_remote_copy(
                snd.at[v, to], rcv.at[v, gy], a_send.at[v], a_recv.at[v],
                device_id=(to, gz), device_id_type=MESH,
            ).start()
        return carry

    send_view(0, 0)
    send_margins()
    lax.fori_loop(1, NV, send_view, 0)

    i0 = lax.broadcasted_iota(jnp.int32, (PL, PE), 0)
    i1 = lax.broadcasted_iota(jnp.int32, (PL, PE), 1)
    for v in range(NV):
        am = jnp.zeros((PL, PE), F32)
        for k in range(TAX):
            am = jnp.where(i1 - i0 == k, axial[v, k], am)
        high, low = split(am)
        acat[v * PL : (v + 1) * PL, :] = jnp.concatenate([high, high, low], axis=1)
    j0 = lax.broadcasted_iota(jnp.int32, (PE, PL), 0)
    j1 = lax.broadcasted_iota(jnp.int32, (PE, PL), 1)
    for v in range(NV):
        am = jnp.zeros((PE, PL), F32)
        for k in range(TAX):
            am = jnp.where(j0 - j1 == k, axial[v, k], am)
        high, low = split(am)
        adj[v] = jnp.concatenate([high, high, low], axis=1)

    def build(v, carry):
        col = lax.broadcasted_iota(jnp.int32, (1, W), 1)
        at = col % RW
        for s in range(PEERS):
            at = jnp.where(col // RW == s, at + order[v, s] * RW, at)
        for b in range(W // 64):
            d = lax.broadcasted_iota(jnp.int32, (64, W), 0) + (b * 64 + HY) - at
            q = jnp.zeros((64, W), F32)
            for i in range(TLAT):
                q = jnp.where(d == i, lat[v, 1, i], q)
            high, low = split(q)
            qh[v, b * 64 : (b + 1) * 64, :] = high
            ql[v, b * 64 : (b + 1) * 64, :] = low
        return carry

    lax.fori_loop(0, NV, build, 0)

    for side in range(2):

        @pl.when(has_z[1 - side])
        def _():
            z_copy(side, 0).wait_recv()

        @pl.when(on_chip[1 - side])
        def _():
            z_copy(side, 1).wait_recv()
            z_copy(side, 2).wait_recv()

        for ys in range(2):

            @pl.when(across[1 - side] & has_y[1 - ys])
            def _():
                d_copy(side, ys).wait_recv()

    def axial_row(y, carry):
        high, low = split(ext[y])
        axb[y] = dot(acat[...], jnp.concatenate([high, low, high], axis=0))
        return carry

    lax.fori_loop(0, RE, axial_row, 0, unroll=4)

    def row_tile(t, carry):
        v = t // 2
        taps = [lat[v, 0, j] for j in range(TLAT)]
        at = pl.multiple_of(t * 16, 16)
        m = pl.multiple_of((t % 2) * 16, 16)
        for c in range(W // 128):
            cols = slice(c * 128, (c + 1) * 128)
            rows = [axb[y, pl.ds(at, 16), cols] for y in range(RE)]
            for y in range(RW):
                acc = taps[0] * rows[y]
                for j in range(1, TLAT):
                    acc = acc + taps[j] * rows[y + j]
                high, low = split(acc)
                lh[v, pl.ds(y * PL + m, 16), cols] = high
                ll[v, pl.ds(y * PL + m, 16), cols] = low
        return carry

    lax.fori_loop(0, NV * 2, row_tile, 0)

    def col_view(v, carry):
        for n in range(2):
            cols = slice(n * 256, (n + 1) * 256)
            res = dot(lh[v], qh[v, :, cols]) + dot(ll[v], qh[v, :, cols]) + dot(lh[v], ql[v, :, cols])
            bl[v, 2 * n] = res[:, :128]
            bl[v, 2 * n + 1] = res[:, 128:]
        return carry

    lax.fori_loop(0, NV, col_view, 0)

    def back_view(v):
        pltpu.make_async_copy(
            rcv.at[v, pl.ds(0, PEERS - 1)], rcv.at[v, pl.ds(0, PEERS - 1)], a_recv.at[v]
        ).wait()

        def group(g, inner):
            for s in range(PEERS // 8):
                cols = slice(s * 128, (s + 1) * 128)
                vals = swap_chunks([rcv[v, s * 8 + k, g] for k in range(8)], RW)
                for z in range(8):
                    den = bl[v, s, pl.ds(g * 8 + z, RW, stride=PL), :]
                    high, low = split(vals[z] / den)
                    at = pl.multiple_of(g * 128 + z * 16, 16)
                    rh[pl.ds(at, 16), cols] = high
                    rl[pl.ds(at, 16), cols] = low
            return inner

        lax.fori_loop(0, ZG, group, 0)
        for n in range(2):
            rows = slice(n * 256, (n + 1) * 256)
            res = dot_nt(rh[...], qh[v, rows, :]) + dot_nt(rl[...], qh[v, rows, :]) + dot_nt(rh[...], ql[v, rows, :])
            bl[v, 2 * n] = res[:, :128]
            bl[v, 2 * n + 1] = res[:, 128:]
        taps = [lat[v, 0, j] for j in range(TLAT)]

        def spread(h, inner):
            for c in range(W // 128):
                cols = slice(c * 128, (c + 1) * 128)
                rows = [bl[v, c, pl.ds(h * 256 + y, 16, stride=RW), :] for y in range(RW)]
                for y in range(RE):
                    acc = None
                    for j in range(TLAT):
                        if 0 <= y - j < RW:
                            term = taps[j] * rows[y - j]
                            acc = term if acc is None else acc + term
                    high, low = split(acc)
                    at = pl.multiple_of(h * 16, 16)
                    tt[y, pl.ds(at, 16), cols] = high
                    tt[y, pl.ds(PL + at, 16), cols] = low
                    tt[y, pl.ds(2 * PL + at, 16), cols] = high
            return inner

        lax.fori_loop(0, 2, spread, 0)

    def axial_back(v, first, start, stop):
        def row(y, carry):
            term = dot(adj[v], tt[y])
            gb[y] = term if first else gb[y] + term
            return carry

        lax.fori_loop(start, stop, row, 0, unroll=4)

    def whole_view(v, carry):
        back_view(v)
        axial_back(v, False, 0, RE)
        return carry

    back_view(0)
    axial_back(0, True, 0, RE)
    lax.fori_loop(1, NV - 1, whole_view, 0)
    back_view(NV - 1)

    parts = ((0, HY), (HY + RW, RE), (HY, HY + RW))

    def zb_copy(side, part):
        src = (slice(0, HZ), slice(HZ + PL, PE))[side]
        rows = slice(*parts[part])
        return pltpu.make_async_remote_copy(
            gb.at[rows, src], zr.at[side, rows], zb_send.at[side, part], zb_recv.at[side, part],
            device_id=(gy, (dn_z, up_z)[side]), device_id_type=MESH,
        )

    def db_copy(zs, ys):
        rows = (slice(0, HY), slice(HY + RW, RE))[ys]
        src = (slice(0, HZ), slice(HZ + PL, PE))[zs]
        return pltpu.make_async_remote_copy(
            gb.at[rows, src], dr.at[zs, ys], db_send.at[zs, ys], db_recv.at[zs, ys],
            device_id=((dn_y, up_y)[ys], (dn_z, up_z)[zs]), device_id_type=MESH,
        )

    def zb_start(part):
        for side in range(2):

            @pl.when((has_z if part == 2 else on_chip)[side])
            def _():
                zb_copy(side, part).start()

    def zb_add(part):
        for side in range(2):

            @pl.when((has_z if part == 2 else on_chip)[1 - side])
            def _():
                zb_copy(side, part).wait_recv()
                at = (slice(PL, PL + HZ), slice(HZ, 2 * HZ))[side]
                for y in range(*parts[part]):
                    gb[y, at] = gb[y, at] + zr[side, y]

    for part in range(2):
        axial_back(NV - 1, False, *parts[part])
        zb_start(part)
    for zs in range(2):
        for ys in range(2):

            @pl.when(across[zs] & has_y[ys])
            def _():
                db_copy(zs, ys).start()

    for part in range(2):
        zb_add(part)

    def yb_copy(side):
        src = (slice(0, HY), slice(HY + RW, RE))[side]
        return pltpu.make_async_remote_copy(
            gb.at[src, HZ : HZ + PL], yr.at[side], yb_send.at[side], yb_recv.at[side],
            device_id=((dn_y, up_y)[side], gz), device_id_type=MESH,
        )

    for side in range(2):

        @pl.when(has_y[side])
        def _():
            yb_copy(side).start()

    axial_back(NV - 1, False, *parts[2])
    zb_start(2)
    zb_add(2)

    def finish(rows):
        for c in range(CC):
            cols = slice(c * 128, (c + 1) * 128)
            for y in rows:
                est_v[c, pl.ds(y, PL, stride=RW), :] = ext[HY + y, HZ : HZ + PL, cols] * (
                    gb[HY + y, HZ : HZ + PL, cols] * (1.0 / NV)
                )

    finish(range(HY, RW - HY))
    for side in range(2):

        @pl.when(has_y[1 - side])
        def _():
            yb_copy(side).wait_recv()
            base = (RW, HY)[side]
            for y in range(HY):
                gb[base + y, HZ : HZ + PL] = gb[base + y, HZ : HZ + PL] + yr[side, y]

        for zs in range(2):

            @pl.when(across[1 - zs] & has_y[1 - side])
            def _():
                db_copy(zs, side).wait_recv()
                base = (RW, HY)[side]
                at = (slice(PL, PL + HZ), slice(HZ, 2 * HZ))[zs]
                for y in range(HY):
                    gb[base + y, at] = gb[base + y, at] + dr[zs, side, y]

    finish([*range(HY), *range(RW - HY, RW)])
    outs = []
    for c in range(CC):
        cols = slice(c * 128, (c + 1) * 128)
        outs.append(pltpu.make_async_copy(est_v.at[c], out_ref.at[:, cols], lsem.at[NV + c]))
        outs[-1].start()
    for copy in outs:
        copy.wait()

    for side in range(2):

        @pl.when(has_y[side])
        def _():
            y_copy(side).wait_send()
            yb_copy(side).wait_send()

        @pl.when(has_z[side])
        def _():
            z_copy(side, 0).wait_send()
            zb_copy(side, 2).wait_send()

        @pl.when(on_chip[side])
        def _():
            for part in range(2):
                z_copy(side, 1 + part).wait_send()
                zb_copy(side, part).wait_send()

        for ys in range(2):

            @pl.when(across[side] & has_y[ys])
            def _():
                d_copy(side, ys).wait_send()
                db_copy(side, ys).wait_send()

    for v in range(NV):
        pltpu.make_async_copy(
            snd.at[v, pl.ds(0, PEERS - 1)], snd.at[v, pl.ds(0, PEERS - 1)], a_send.at[v]
        ).wait()


def local(estimate, observed, tile_order, lateral_taps, axial_taps):
    rows = PL * RW
    smem = pl.BlockSpec(memory_space=pltpu.SMEM)
    hbm = pl.BlockSpec(memory_space=pl.ANY)
    dma = pltpu.SemaphoreType.DMA
    out = pl.pallas_call(
        kernel,
        out_shape=jax.ShapeDtypeStruct((rows, W), F32),
        in_specs=[hbm, hbm, smem, smem, smem],
        out_specs=hbm,
        scratch_shapes=[
            pltpu.VMEM((CC, rows, 128), F32),
            pltpu.VMEM((NV, rows, W), F32),
            pltpu.VMEM((NV, PEERS, ZG, RW, 128), F32),
            pltpu.VMEM((NV, PEERS, ZG, RW, 128), F32),
            pltpu.VMEM((RE, PE, W), F32),
            pltpu.VMEM((RE, NV * PL, W), F32),
            pltpu.VMEM((NV, rows, W), BF16),
            pltpu.VMEM((NV, rows, W), BF16),
            pltpu.VMEM((NV, CC, rows, 128), F32),
            pltpu.VMEM((NV, W, W), BF16),
            pltpu.VMEM((NV, W, W), BF16),
            pltpu.VMEM((rows, W), BF16),
            pltpu.VMEM((rows, W), BF16),
            pltpu.VMEM((RE, 3 * PL, W), BF16),
            pltpu.VMEM((NV * PL, 3 * PE), BF16),
            pltpu.VMEM((NV, PE, 3 * PL), BF16),
            pltpu.VMEM((RE, PE, W), F32),
            pltpu.VMEM((2, RE, HZ, W), F32),
            pltpu.VMEM((2, HY, PL, W), F32),
            pltpu.VMEM((2, 2, HY, HZ, W), F32),
            dma((NV + CC,)),
            dma((NV,)),
            dma((NV,)),
            dma((2,)),
            dma((2,)),
            dma((2, 3)),
            dma((2, 3)),
            dma((2, 3)),
            dma((2, 3)),
            dma((2,)),
            dma((2,)),
            dma((2, 2)),
            dma((2, 2)),
            dma((2, 2)),
            dma((2, 2)),
        ],
        compiler_params=pltpu.CompilerParams(
            collective_id=0, has_side_effects=True, vmem_limit_bytes=60 << 20
        ),
    )(
        estimate.reshape(rows, W),
        observed.reshape(NV, rows, W),
        tile_order,
        lateral_taps,
        axial_taps,
    )
    return out.reshape(PL, RW, W)


def solution(mesh):
    return jax.shard_map(
        local,
        mesh=mesh,
        in_specs=(P("gz", "gy", None), P(None, "gz", "gy", None), P(), P(), P()),
        out_specs=P("gz", "gy", None),
        check_vma=False,
    )
```

```python
import functools

import jax
import jax.numpy as jnp
from jax import lax
from jax.experimental import pallas as pl
from jax.experimental.pallas import tpu as pltpu
from jax.sharding import PartitionSpec as P

MESH = pl.DeviceIdType.MESH
F32 = jnp.float32
BF16 = jnp.bfloat16

NV = 4
TAX = 33
TLAT = 9
PL = 32
RW = 16
W = 512
PEERS = 32
SLABS = 4
HZ = TAX // 2
HY = TLAT // 2
PE = PL + 2 * HZ
RE = RW + 2 * HY
ZG = PL // 8
CC = W // 128


PLANE = (
    (1, 0), (0, 1), (3, 0), (0, 3), (2, 1), (1, 2), (2, 3), (3, 2), (1, 1), (3, 3), (1, 3), (3, 1), (2, 0), (0, 2), (2, 2),
)
ORDER = ((0, 0, 1),) + tuple((dz, dy, dx) for dz, dy in PLANE for dx in (1, 0))


KEPT = (0, 1, 2, 3, 12, 13, 14, 15, 8, 9, 10, 11, 4, 5, 6, 7)
PLACE = tuple(KEPT.index(y) for y in range(RW))
EDGE = (*range(HY), *range(HY + RW, RE))
INNER = tuple(range(HY, HY + RW))


def split(value):
    high = value.astype(BF16)
    return high, (value - high.astype(F32)).astype(BF16)


def dot(a, b):
    return jnp.dot(a, b, preferred_element_type=F32)


def dot_nt(a, b):
    return lax.dot_general(a, b, (((1,), (1,)), ((), ())), preferred_element_type=F32)


def swap_chunks(vals, chunk):
    span = vals[0].shape[-1]
    which = lax.broadcasted_iota(jnp.int32, vals[0].shape, vals[0].ndim - 1) // chunk
    for b in (4, 2, 1):
        low = (which & b) == 0
        new = list(vals)
        for k in range(8):
            if k & b:
                continue
            new[k] = jnp.where(low, vals[k], pltpu.roll(vals[k | b], b * chunk, 1))
            new[k | b] = jnp.where(low, pltpu.roll(vals[k], span - b * chunk, 1), vals[k | b])
        vals = new
    return vals


def kernel(
    est_hbm, obs_hbm, order, lat, axial, out_ref,
    est_v, obs_v, snd, rcv, ext, axb, lh, ll, bl, qh, ql, rh, rl, tt, acat, adj, gb, zr, yr, dr,
    lsem, a_send, a_recv, y_send, y_recv, z_send, z_recv, zb_send, zb_recv, yb_send, yb_recv,
    d_send, d_recv, db_send, db_recv,
):
    gy = lax.axis_index("gy")
    gz = lax.axis_index("gz")
    cz, cy, cx = gy // 8, (gy // 2) % 4, gy % 2

    est_in = [
        pltpu.make_async_copy(est_hbm.at[:, c * 128 : (c + 1) * 128], est_v.at[c], lsem.at[NV + c])
        for c in range(CC)
    ]
    for copy in est_in:
        copy.start()
    for v in range(NV):
        pltpu.make_async_copy(obs_hbm.at[v], obs_v.at[v], lsem.at[v]).start()

    def peer(dz, dy, dx):
        return ((cz + dz) % 4) * 8 + ((cy + dy) % 4) * 2 + (cx + dx) % 2

    bar = pltpu.get_barrier_semaphore()

    for offset in ORDER:
        pl.semaphore_signal(bar, inc=1, device_id=(peer(*offset), gz), device_id_type=MESH)
    up_z, dn_z = (gz + 1) % SLABS, (gz + SLABS - 1) % SLABS
    up_y, dn_y = (gy + 1) % PEERS, (gy + PEERS - 1) % PEERS
    for other in (up_z, dn_z):
        pl.semaphore_signal(bar, inc=1, device_id=(gy, other), device_id_type=MESH)

    middle = gz * (SLABS - 1 - gz) // 2

    @pl.when(middle == 1)
    def _():
        for other in (up_y, dn_y):
            pl.semaphore_signal(
                bar, inc=1, device_id=(other, SLABS - 1 - gz), device_id_type=MESH
            )

    for c, copy in enumerate(est_in):
        copy.wait()
        for y in range(RW):
            ext[HY + y, HZ : HZ + PL, c * 128 : (c + 1) * 128] = est_v[c, pl.ds(y, PL, stride=RW), :]

    @pl.when(gy == 0)
    def _():
        ext[0:HY, HZ : HZ + PL, :] = jnp.zeros((HY, PL, W), F32)

    @pl.when(gy == PEERS - 1)
    def _():
        ext[HY + RW : RE, HZ : HZ + PL, :] = jnp.zeros((HY, PL, W), F32)

    @pl.when(gz == 0)
    def _():
        ext[:, 0:HZ, :] = jnp.zeros((RE, HZ, W), F32)

    @pl.when(gz == SLABS - 1)
    def _():
        ext[:, HZ + PL : PE, :] = jnp.zeros((RE, HZ, W), F32)

    for z_edge, planes in ((1, slice(HZ + PL, PE)), (2, slice(0, HZ))):
        for y_edge, rows in ((0, slice(0, HY)), (PEERS - 1, slice(HY + RW, RE))):

            @pl.when((gz == z_edge) & (gy == y_edge))
            def _():
                ext[rows, planes, :] = jnp.zeros((HY, HZ, W), F32)

    pl.semaphore_wait(bar, PEERS - 1 + 2 + 2 * middle)

    def y_copy(side):
        src = (slice(HY, 2 * HY), slice(RW, RW + HY))[side]
        dst = (slice(HY + RW, RE), slice(0, HY))[side]
        return pltpu.make_async_remote_copy(
            ext.at[src, HZ : HZ + PL], ext.at[dst, HZ : HZ + PL], y_send.at[side], y_recv.at[side],
            device_id=((dn_y, up_y)[side], gz), device_id_type=MESH,
        )

    def z_copy(side, part):
        rows = (slice(HY, HY + RW), slice(0, HY), slice(HY + RW, RE))[part]
        src = (slice(HZ, 2 * HZ), slice(PL, PL + HZ))[side]
        dst = (slice(HZ + PL, PE), slice(0, HZ))[side]
        return pltpu.make_async_remote_copy(
            ext.at[rows, src], ext.at[rows, dst], z_send.at[side, part], z_recv.at[side, part],
            device_id=(gy, (dn_z, up_z)[side]), device_id_type=MESH,
        )

    def d_copy(zs, ys):
        rows = (slice(HY, 2 * HY), slice(RW, RW + HY))[ys]
        to_rows = (slice(HY + RW, RE), slice(0, HY))[ys]
        src = (slice(HZ, 2 * HZ), slice(PL, PL + HZ))[zs]
        dst = (slice(HZ + PL, PE), slice(0, HZ))[zs]
        return pltpu.make_async_remote_copy(
            ext.at[rows, src], ext.at[to_rows, dst], d_send.at[zs, ys], d_recv.at[zs, ys],
            device_id=((dn_y, up_y)[ys], (dn_z, up_z)[zs]), device_id_type=MESH,
        )

    on_chip = (gz % 2 == 1, gz % 2 == 0)
    across = (gz == 2, gz == 1)
    has_y = (gy > 0, gy < PEERS - 1)
    has_z = (gz > 0, gz < SLABS - 1)
    for side in range(2):

        @pl.when(has_y[side])
        def _():
            y_copy(side).start()

        @pl.when(has_z[side])
        def _():
            z_copy(side, 0).start()

    for zs in range(2):
        for ys in range(2):

            @pl.when(across[zs] & has_y[ys])
            def _():
                d_copy(zs, ys).start()

    def send_margins():
        for side in range(2):

            @pl.when(has_y[1 - side])
            def _():
                y_copy(side).wait_recv()

        for side in range(2):

            @pl.when(on_chip[side])
            def _():
                z_copy(side, 1).start()
                z_copy(side, 2).start()

    upper = lax.broadcasted_iota(jnp.int32, (8, 128), 0) < HY

    def parts_of(v, ref, at):
        if isinstance(v, int) and v == NV - 1:
            return [(ref.at[v, at, :, h * 8 : (h + 1) * 8], v + h) for h in range(2)]
        return [(ref.at[v, at], v)]

    def send_view(v, carry):
        pltpu.make_async_copy(obs_hbm.at[v], obs_v.at[v], lsem.at[v]).wait()
        for g in range(ZG):
            for c in range(4):
                t = obs_v[v, g * 128 : (g + 1) * 128, c * 128 : (c + 1) * 128].T
                for d in range(8):
                    first = t[d * RW : d * RW + 8, :]
                    second = t[d * RW + 8 : (d + 1) * RW, :]
                    snd[v, c * 8 + d, g, 0:8] = jnp.where(upper, first, second)
                    snd[v, c * 8 + d, g, 8:RW] = jnp.where(upper, second, first)
        rcv[v, gy] = snd[v, gy]

        for h in range(len(parts_of(v, snd, 0))):
            for offset in ORDER:
                to = peer(*offset)
                src, n = parts_of(v, snd, to)[h]
                dst, _ = parts_of(v, rcv, gy)[h]
                pltpu.make_async_remote_copy(
                    src, dst, a_send.at[n], a_recv.at[n], device_id=(to, gz), device_id_type=MESH
                ).start()
        return carry

    send_view(0, 0)
    send_margins()
    lax.fori_loop(1, NV - 1, send_view, 0)
    send_view(NV - 1, 0)

    i0 = lax.broadcasted_iota(jnp.int32, (PL, PE), 0)
    i1 = lax.broadcasted_iota(jnp.int32, (PL, PE), 1)
    for v in range(NV):
        am = jnp.zeros((PL, PE), F32)
        for k in range(TAX):
            am = jnp.where(i1 - i0 == k, axial[v, k], am)
        high, low = split(am)
        acat[v * PL : (v + 1) * PL, :] = jnp.concatenate([high, high, low], axis=1)
    j0 = lax.broadcasted_iota(jnp.int32, (PE, PL), 0)
    j1 = lax.broadcasted_iota(jnp.int32, (PE, PL), 1)
    for v in range(NV):
        am = jnp.zeros((PE, PL), F32)
        for k in range(TAX):
            am = jnp.where(j0 - j1 == k, axial[v, k], am)
        high, low = split(am)
        adj[v] = jnp.concatenate([high, high, low], axis=1)

    def build(v, carry):
        col = lax.broadcasted_iota(jnp.int32, (1, W), 1)
        at = col % RW
        for s in range(PEERS):
            at = jnp.where(col // RW == s, at + order[v, s] * RW, at)
        for b in range(W // 64):
            d = lax.broadcasted_iota(jnp.int32, (64, W), 0) + (b * 64 + HY) - at
            q = jnp.zeros((64, W), F32)
            for i in range(TLAT):
                q = jnp.where(d == i, lat[v, 1, i], q)
            high, low = split(q)
            qh[v, b * 64 : (b + 1) * 64, :] = high
            ql[v, b * 64 : (b + 1) * 64, :] = low
        return carry

    lax.fori_loop(0, NV, build, 0)

    for side in range(2):

        @pl.when(has_z[1 - side])
        def _():
            z_copy(side, 0).wait_recv()

        @pl.when(on_chip[1 - side])
        def _():
            z_copy(side, 1).wait_recv()
            z_copy(side, 2).wait_recv()

        for ys in range(2):

            @pl.when(across[1 - side] & has_y[1 - ys])
            def _():
                d_copy(side, ys).wait_recv()

    def axial_row(y, carry):
        high, low = split(ext[y])
        axb[y] = dot(acat[...], jnp.concatenate([high, low, high], axis=0))
        return carry

    lax.fori_loop(0, RE, axial_row, 0, unroll=4)

    def row_tile(t, carry):
        v = t // 2
        taps = [lat[v, 0, j] for j in range(TLAT)]
        at = pl.multiple_of(t * 16, 16)
        m = pl.multiple_of((t % 2) * 16, 16)
        for c in range(W // 128):
            cols = slice(c * 128, (c + 1) * 128)
            rows = [axb[y, pl.ds(at, 16), cols] for y in range(RE)]
            for y in range(RW):
                acc = taps[0] * rows[y]
                for j in range(1, TLAT):
                    acc = acc + taps[j] * rows[y + j]
                high, low = split(acc)
                lh[v, pl.ds(PLACE[y] * PL + m, 16), cols] = high
                ll[v, pl.ds(PLACE[y] * PL + m, 16), cols] = low
        return carry

    lax.fori_loop(0, NV * 2, row_tile, 0)

    def col_view(v, carry):
        for n in range(2):
            cols = slice(n * 256, (n + 1) * 256)
            res = dot(lh[v], qh[v, :, cols]) + dot(ll[v], qh[v, :, cols]) + dot(lh[v], ql[v, :, cols])
            bl[v, 2 * n] = res[:, :128]
            bl[v, 2 * n + 1] = res[:, 128:]
        return carry

    lax.fori_loop(0, NV, col_view, 0)

    def arrived(v):
        for h in range(len(parts_of(v, rcv, 0))):
            yield lambda h=h: pltpu.make_async_copy(
                parts_of(v, rcv, pl.ds(0, PEERS - 1))[h][0],
                parts_of(v, rcv, pl.ds(0, PEERS - 1))[h][0],
                a_recv.at[parts_of(v, rcv, 0)[h][1]],
            ).wait()

    def ratio(v, halves):
        def group(g, inner):
            for h in halves:
                for s in range(PEERS // 8):
                    cols = slice(s * 128, (s + 1) * 128)
                    vals = swap_chunks(
                        [rcv[v, s * 8 + k, g, h * 8 : (h + 1) * 8] for k in range(8)], RW
                    )
                    vals = [
                        vals[z] / bl[v, s, pl.ds(h * 256 + g * 8 + z, 8, stride=PL), :]
                        for z in range(8)
                    ]
                    for z in range(0, 8, 2):
                        high, low = split(jnp.concatenate(vals[z : z + 2], axis=0))
                        at = pl.multiple_of(h * 256 + g * 64 + z * 8, 16)
                        rh[pl.ds(at, 16), cols] = high
                        rl[pl.ds(at, 16), cols] = low
            return inner

        lax.fori_loop(0, ZG, group, 0)

    def columns_back(v, start, stop):
        at = slice(start, stop)
        for n in range(2):
            rows = slice(n * 256, (n + 1) * 256)
            res = (
                dot_nt(rh[at], qh[v, rows, :]) + dot_nt(rl[at], qh[v, rows, :]) + dot_nt(rh[at], ql[v, rows, :])
            )
            bl[v, 2 * n, at] = res[:, :128]
            bl[v, 2 * n + 1, at] = res[:, 128:]

    def rows_back(v, outs):
        taps = [lat[v, 0, j] for j in range(TLAT)]
        used = sorted({y - j for y in outs for j in range(TLAT) if 0 <= y - j < RW})

        def spread(h, inner):
            for c in range(W // 128):
                cols = slice(c * 128, (c + 1) * 128)
                rows = {
                    y: bl[v, c, pl.ds(PLACE[y] // 8 * 256 + h * 128 + PLACE[y] % 8, 16, stride=8), :]
                    for y in used
                }
                for y in outs:
                    acc = None
                    for j in range(TLAT):
                        if 0 <= y - j < RW:
                            term = taps[j] * rows[y - j]
                            acc = term if acc is None else acc + term
                    high, low = split(acc)
                    at = pl.multiple_of(h * 16, 16)
                    tt[y, pl.ds(at, 16), cols] = high
                    tt[y, pl.ds(PL + at, 16), cols] = low
                    tt[y, pl.ds(2 * PL + at, 16), cols] = high
            return inner

        lax.fori_loop(0, 2, spread, 0)

    def axial_back(v, first, start, stop):
        def row(y, carry):
            term = dot(adj[v], tt[y])
            gb[y] = term if first else gb[y] + term
            return carry

        lax.fori_loop(start, stop, row, 0, unroll=4)

    def whole_view(v, first):
        for wait in arrived(v):
            wait()
        ratio(v, (0, 1))
        columns_back(v, 0, 512)
        rows_back(v, range(RE))
        axial_back(v, first, 0, RE)

    def next_view(v, carry):
        whole_view(v, False)
        return carry

    whole_view(0, True)
    lax.fori_loop(1, NV - 1, next_view, 0)

    last = NV - 1
    edge_in, inner_in = arrived(last)
    edge_in()
    ratio(last, (0,))
    columns_back(last, 0, 256)
    rows_back(last, EDGE)

    parts = ((0, HY), (HY + RW, RE), (HY, HY + RW))

    def zb_copy(side, part):
        src = (slice(0, HZ), slice(HZ + PL, PE))[side]
        rows = slice(*parts[part])
        return pltpu.make_async_remote_copy(
            gb.at[rows, src], zr.at[side, rows], zb_send.at[side, part], zb_recv.at[side, part],
            device_id=(gy, (dn_z, up_z)[side]), device_id_type=MESH,
        )

    def db_copy(zs, ys):
        rows = (slice(0, HY), slice(HY + RW, RE))[ys]
        src = (slice(0, HZ), slice(HZ + PL, PE))[zs]
        return pltpu.make_async_remote_copy(
            gb.at[rows, src], dr.at[zs, ys], db_send.at[zs, ys], db_recv.at[zs, ys],
            device_id=((dn_y, up_y)[ys], (dn_z, up_z)[zs]), device_id_type=MESH,
        )

    def zb_start(part):
        for side in range(2):

            @pl.when((has_z if part == 2 else on_chip)[side])
            def _():
                zb_copy(side, part).start()

    def zb_add(part):
        for side in range(2):

            @pl.when((has_z if part == 2 else on_chip)[1 - side])
            def _():
                zb_copy(side, part).wait_recv()
                at = (slice(PL, PL + HZ), slice(HZ, 2 * HZ))[side]
                for y in range(*parts[part]):
                    gb[y, at] = gb[y, at] + zr[side, y]

    for part in range(2):
        axial_back(last, False, *parts[part])
        zb_start(part)
    for zs in range(2):
        for ys in range(2):

            @pl.when(across[zs] & has_y[ys])
            def _():
                db_copy(zs, ys).start()

    for part in range(2):
        zb_add(part)

    def yb_copy(side):
        src = (slice(0, HY), slice(HY + RW, RE))[side]
        return pltpu.make_async_remote_copy(
            gb.at[src, HZ : HZ + PL], yr.at[side], yb_send.at[side], yb_recv.at[side],
            device_id=((dn_y, up_y)[side], gz), device_id_type=MESH,
        )

    for side in range(2):

        @pl.when(has_y[side])
        def _():
            yb_copy(side).start()

    inner_in()
    ratio(last, (1,))
    columns_back(last, 256, 512)
    rows_back(last, INNER)
    axial_back(last, False, *parts[2])
    zb_start(2)
    zb_add(2)

    def finish(rows):
        for c in range(CC):
            cols = slice(c * 128, (c + 1) * 128)
            for y in rows:
                est_v[c, pl.ds(y, PL, stride=RW), :] = ext[HY + y, HZ : HZ + PL, cols] * (
                    gb[HY + y, HZ : HZ + PL, cols] * (1.0 / NV)
                )

    finish(range(HY, RW - HY))
    for side in range(2):

        @pl.when(has_y[1 - side])
        def _():
            yb_copy(side).wait_recv()
            base = (RW, HY)[side]
            for y in range(HY):
                gb[base + y, HZ : HZ + PL] = gb[base + y, HZ : HZ + PL] + yr[side, y]

        for zs in range(2):

            @pl.when(across[1 - zs] & has_y[1 - side])
            def _():
                db_copy(zs, side).wait_recv()
                base = (RW, HY)[side]
                at = (slice(PL, PL + HZ), slice(HZ, 2 * HZ))[zs]
                for y in range(HY):
                    gb[base + y, at] = gb[base + y, at] + dr[zs, side, y]

    finish([*range(HY), *range(RW - HY, RW)])
    outs = []
    for c in range(CC):
        cols = slice(c * 128, (c + 1) * 128)
        outs.append(pltpu.make_async_copy(est_v.at[c], out_ref.at[:, cols], lsem.at[NV + c]))
        outs[-1].start()
    for copy in outs:
        copy.wait()

    for side in range(2):

        @pl.when(has_y[side])
        def _():
            y_copy(side).wait_send()
            yb_copy(side).wait_send()

        @pl.when(has_z[side])
        def _():
            z_copy(side, 0).wait_send()
            zb_copy(side, 2).wait_send()

        @pl.when(on_chip[side])
        def _():
            for part in range(2):
                z_copy(side, 1 + part).wait_send()
                zb_copy(side, part).wait_send()

        for ys in range(2):

            @pl.when(across[side] & has_y[ys])
            def _():
                d_copy(side, ys).wait_send()
                db_copy(side, ys).wait_send()

    for v in range(NV):
        for block, n in parts_of(v, snd, pl.ds(0, PEERS - 1)):
            pltpu.make_async_copy(block, block, a_send.at[n]).wait()


def local(estimate, observed, tile_order, lateral_taps, axial_taps):
    rows = PL * RW
    smem = pl.BlockSpec(memory_space=pltpu.SMEM)
    hbm = pl.BlockSpec(memory_space=pl.ANY)
    dma = pltpu.SemaphoreType.DMA
    out = pl.pallas_call(
        kernel,
        out_shape=jax.ShapeDtypeStruct((rows, W), F32),
        in_specs=[hbm, hbm, smem, smem, smem],
        out_specs=hbm,
        scratch_shapes=[
            pltpu.VMEM((CC, rows, 128), F32),
            pltpu.VMEM((NV, rows, W), F32),
            pltpu.VMEM((NV, PEERS, ZG, RW, 128), F32),
            pltpu.VMEM((NV, PEERS, ZG, RW, 128), F32),
            pltpu.VMEM((RE, PE, W), F32),
            pltpu.VMEM((RE, NV * PL, W), F32),
            pltpu.VMEM((NV, rows, W), BF16),
            pltpu.VMEM((NV, rows, W), BF16),
            pltpu.VMEM((NV, CC, rows, 128), F32),
            pltpu.VMEM((NV, W, W), BF16),
            pltpu.VMEM((NV, W, W), BF16),
            pltpu.VMEM((rows, W), BF16),
            pltpu.VMEM((rows, W), BF16),
            pltpu.VMEM((RE, 3 * PL, W), BF16),
            pltpu.VMEM((NV * PL, 3 * PE), BF16),
            pltpu.VMEM((NV, PE, 3 * PL), BF16),
            pltpu.VMEM((RE, PE, W), F32),
            pltpu.VMEM((2, RE, HZ, W), F32),
            pltpu.VMEM((2, HY, PL, W), F32),
            pltpu.VMEM((2, 2, HY, HZ, W), F32),
            dma((NV + CC,)),
            dma((NV + 1,)),
            dma((NV + 1,)),
            dma((2,)),
            dma((2,)),
            dma((2, 3)),
            dma((2, 3)),
            dma((2, 3)),
            dma((2, 3)),
            dma((2,)),
            dma((2,)),
            dma((2, 2)),
            dma((2, 2)),
            dma((2, 2)),
            dma((2, 2)),
        ],
        compiler_params=pltpu.CompilerParams(
            collective_id=0, has_side_effects=True, vmem_limit_bytes=60 << 20
        ),
    )(
        estimate.reshape(rows, W),
        observed.reshape(NV, rows, W),
        tile_order,
        lateral_taps,
        axial_taps,
    )
    return out.reshape(PL, RW, W)


def solution(mesh):
    return jax.shard_map(
        local,
        mesh=mesh,
        in_specs=(P("gz", "gy", None), P(None, "gz", "gy", None), P(), P(), P()),
        out_specs=P("gz", "gy", None),
        check_vma=False,
    )
```

```python
import functools

import jax
import jax.numpy as jnp
from jax import lax
from jax.experimental import pallas as pl
from jax.experimental.pallas import tpu as pltpu
from jax.sharding import PartitionSpec as P

MESH = pl.DeviceIdType.MESH
F32 = jnp.float32
BF16 = jnp.bfloat16

NV = 4
TAX = 33
TLAT = 9
PL = 32
RW = 16
W = 512
PEERS = 32
SLABS = 4
HZ = TAX // 2
HY = TLAT // 2
PE = PL + 2 * HZ
RE = RW + 2 * HY
ZG = PL // 8
CC = W // 128


PLANE = (
    (1, 0), (0, 1), (3, 0), (0, 3), (2, 1), (1, 2), (2, 3), (3, 2), (1, 1), (3, 3), (1, 3), (3, 1), (2, 0), (0, 2), (2, 2),
)
ORDER = tuple(
    sorted(
        ((0, 0, 1),) + tuple((dz, dy, dx) for dz, dy in PLANE for dx in (1, 0)),
        key=lambda o: -(min(o[0], 4 - o[0]) + min(o[1], 4 - o[1]) + o[2]),
    )
)


KEPT = (0, 1, 2, 3, 12, 13, 14, 15, 8, 9, 10, 11, 4, 5, 6, 7)
PLACE = tuple(KEPT.index(y) for y in range(RW))
EDGE = (*range(HY), *range(HY + RW, RE))
INNER = tuple(range(HY, HY + RW))


def split(value):
    high = value.astype(BF16)
    return high, (value - high.astype(F32)).astype(BF16)


def dot(a, b):
    return jnp.dot(a, b, preferred_element_type=F32)


def dot_nt(a, b):
    return lax.dot_general(a, b, (((1,), (1,)), ((), ())), preferred_element_type=F32)


def swap_chunks(vals, chunk):
    span = vals[0].shape[-1]
    which = lax.broadcasted_iota(jnp.int32, vals[0].shape, vals[0].ndim - 1) // chunk
    for b in (4, 2, 1):
        low = (which & b) == 0
        new = list(vals)
        for k in range(8):
            if k & b:
                continue
            new[k] = jnp.where(low, vals[k], pltpu.roll(vals[k | b], b * chunk, 1))
            new[k | b] = jnp.where(low, pltpu.roll(vals[k], span - b * chunk, 1), vals[k | b])
        vals = new
    return vals


def kernel(
    est_hbm, obs_hbm, order, lat, axial, out_ref,
    est_v, obs_v, snd, rcv, ext, axb, lh, ll, bl, qh, ql, rh, rl, tt, acat, adj, gb, zr, yr, dr,
    lsem, a_send, a_recv, y_send, y_recv, z_send, z_recv, zb_send, zb_recv, yb_send, yb_recv,
    d_send, d_recv, db_send, db_recv,
):
    gy = lax.axis_index("gy")
    gz = lax.axis_index("gz")
    cz, cy, cx = gy // 8, (gy // 2) % 4, gy % 2

    est_in = [
        pltpu.make_async_copy(est_hbm.at[:, c * 128 : (c + 1) * 128], est_v.at[c], lsem.at[NV + c])
        for c in range(CC)
    ]
    for copy in est_in:
        copy.start()
    for v in range(NV):
        pltpu.make_async_copy(obs_hbm.at[v], obs_v.at[v], lsem.at[v]).start()

    def peer(dz, dy, dx):
        return ((cz + dz) % 4) * 8 + ((cy + dy) % 4) * 2 + (cx + dx) % 2

    bar = pltpu.get_barrier_semaphore()

    for offset in ORDER:
        pl.semaphore_signal(bar, inc=1, device_id=(peer(*offset), gz), device_id_type=MESH)
    up_z, dn_z = (gz + 1) % SLABS, (gz + SLABS - 1) % SLABS
    up_y, dn_y = (gy + 1) % PEERS, (gy + PEERS - 1) % PEERS
    for other in (up_z, dn_z):
        pl.semaphore_signal(bar, inc=1, device_id=(gy, other), device_id_type=MESH)

    middle = gz * (SLABS - 1 - gz) // 2

    @pl.when(middle == 1)
    def _():
        for other in (up_y, dn_y):
            pl.semaphore_signal(
                bar, inc=1, device_id=(other, SLABS - 1 - gz), device_id_type=MESH
            )

    for c, copy in enumerate(est_in):
        copy.wait()
        for y in range(RW):
            ext[HY + y, HZ : HZ + PL, c * 128 : (c + 1) * 128] = est_v[c, pl.ds(y, PL, stride=RW), :]

    @pl.when(gy == 0)
    def _():
        ext[0:HY, HZ : HZ + PL, :] = jnp.zeros((HY, PL, W), F32)

    @pl.when(gy == PEERS - 1)
    def _():
        ext[HY + RW : RE, HZ : HZ + PL, :] = jnp.zeros((HY, PL, W), F32)

    @pl.when(gz == 0)
    def _():
        ext[:, 0:HZ, :] = jnp.zeros((RE, HZ, W), F32)

    @pl.when(gz == SLABS - 1)
    def _():
        ext[:, HZ + PL : PE, :] = jnp.zeros((RE, HZ, W), F32)

    for z_edge, planes in ((1, slice(HZ + PL, PE)), (2, slice(0, HZ))):
        for y_edge, rows in ((0, slice(0, HY)), (PEERS - 1, slice(HY + RW, RE))):

            @pl.when((gz == z_edge) & (gy == y_edge))
            def _():
                ext[rows, planes, :] = jnp.zeros((HY, HZ, W), F32)

    pl.semaphore_wait(bar, PEERS - 1 + 2 + 2 * middle)

    def y_copy(side):
        src = (slice(HY, 2 * HY), slice(RW, RW + HY))[side]
        dst = (slice(HY + RW, RE), slice(0, HY))[side]
        return pltpu.make_async_remote_copy(
            ext.at[src, HZ : HZ + PL], ext.at[dst, HZ : HZ + PL], y_send.at[side], y_recv.at[side],
            device_id=((dn_y, up_y)[side], gz), device_id_type=MESH,
        )

    def z_copy(side, part):
        rows = (slice(HY, HY + RW), slice(0, HY), slice(HY + RW, RE))[part]
        src = (slice(HZ, 2 * HZ), slice(PL, PL + HZ))[side]
        dst = (slice(HZ + PL, PE), slice(0, HZ))[side]
        return pltpu.make_async_remote_copy(
            ext.at[rows, src], ext.at[rows, dst], z_send.at[side, part], z_recv.at[side, part],
            device_id=(gy, (dn_z, up_z)[side]), device_id_type=MESH,
        )

    def d_copy(zs, ys):
        rows = (slice(HY, 2 * HY), slice(RW, RW + HY))[ys]
        to_rows = (slice(HY + RW, RE), slice(0, HY))[ys]
        src = (slice(HZ, 2 * HZ), slice(PL, PL + HZ))[zs]
        dst = (slice(HZ + PL, PE), slice(0, HZ))[zs]
        return pltpu.make_async_remote_copy(
            ext.at[rows, src], ext.at[to_rows, dst], d_send.at[zs, ys], d_recv.at[zs, ys],
            device_id=((dn_y, up_y)[ys], (dn_z, up_z)[zs]), device_id_type=MESH,
        )

    on_chip = (gz % 2 == 1, gz % 2 == 0)
    across = (gz == 2, gz == 1)
    has_y = (gy > 0, gy < PEERS - 1)
    has_z = (gz > 0, gz < SLABS - 1)
    def y_piece(side, p):
        src = (HY, RW)[side]
        dst = (HY + RW, 0)[side]
        at = slice(HZ + p * 8, HZ + p * 8 + 8)

        @pl.when(has_y[side])
        def _():
            pltpu.make_async_remote_copy(
                ext.at[src : src + HY, at], ext.at[dst : dst + HY, at], y_send.at[side], y_recv.at[side],
                device_id=((dn_y, up_y)[side], gz), device_id_type=MESH,
            ).start()

    def z_piece(side, p):
        rows = slice(HY + 4 * p, HY + 4 * p + 4)
        src = (slice(HZ, 2 * HZ), slice(PL, PL + HZ))[side]
        dst = (slice(HZ + PL, PE), slice(0, HZ))[side]

        @pl.when(has_z[side])
        def _():
            pltpu.make_async_remote_copy(
                ext.at[rows, src], ext.at[rows, dst], z_send.at[side, 0], z_recv.at[side, 0],
                device_id=(gy, (dn_z, up_z)[side]), device_id_type=MESH,
            ).start()

    def d_piece(zs, ys):
        @pl.when(across[zs] & has_y[ys])
        def _():
            d_copy(zs, ys).start()

    y_pieces = [functools.partial(y_piece, side, p) for p in range(4) for side in range(2)]
    z_pieces = [functools.partial(z_piece, side, p) for p in range(4) for side in range(2)]
    z_pieces += [functools.partial(d_piece, a, b) for a in range(2) for b in range(2)]

    def send_margins():
        for side in range(2):

            @pl.when(has_y[1 - side])
            def _():
                y_copy(side).wait_recv()

        for side in range(2):

            @pl.when(on_chip[side])
            def _():
                z_copy(side, 1).start()
                z_copy(side, 2).start()

    upper = lax.broadcasted_iota(jnp.int32, (8, 128), 0) < HY

    def parts_of(v, ref, at):
        if isinstance(v, int) and v == NV - 1:
            return [(ref.at[v, at, :, h * 8 : (h + 1) * 8], v + h) for h in range(2)]
        return [(ref.at[v, at], v)]

    def send_view(v, carry, between=()):
        between = list(between)
        pltpu.make_async_copy(obs_hbm.at[v], obs_v.at[v], lsem.at[v]).wait()
        for g in range(ZG):
            for c in range(4):
                t = obs_v[v, g * 128 : (g + 1) * 128, c * 128 : (c + 1) * 128].T
                for d in range(8):
                    first = t[d * RW : d * RW + 8, :]
                    second = t[d * RW + 8 : (d + 1) * RW, :]
                    snd[v, c * 8 + d, g, 0:8] = jnp.where(upper, first, second)
                    snd[v, c * 8 + d, g, 8:RW] = jnp.where(upper, second, first)
        rcv[v, gy] = snd[v, gy]

        for h in range(len(parts_of(v, snd, 0))):
            for offset in ORDER:
                if between:
                    between.pop(0)()
                to = peer(*offset)
                src, n = parts_of(v, snd, to)[h]
                dst, _ = parts_of(v, rcv, gy)[h]
                pltpu.make_async_remote_copy(
                    src, dst, a_send.at[n], a_recv.at[n], device_id=(to, gz), device_id_type=MESH
                ).start()
        return carry

    send_view(0, 0, y_pieces + z_pieces)
    send_view(1, 0)
    send_margins()
    lax.fori_loop(2, NV - 1, send_view, 0)
    send_view(NV - 1, 0)

    i0 = lax.broadcasted_iota(jnp.int32, (PL, PE), 0)
    i1 = lax.broadcasted_iota(jnp.int32, (PL, PE), 1)
    for v in range(NV):
        am = jnp.zeros((PL, PE), F32)
        for k in range(TAX):
            am = jnp.where(i1 - i0 == k, axial[v, k], am)
        high, low = split(am)
        acat[v * PL : (v + 1) * PL, :] = jnp.concatenate([high, high, low], axis=1)
    j0 = lax.broadcasted_iota(jnp.int32, (PE, PL), 0)
    j1 = lax.broadcasted_iota(jnp.int32, (PE, PL), 1)
    for v in range(NV):
        am = jnp.zeros((PE, PL), F32)
        for k in range(TAX):
            am = jnp.where(j0 - j1 == k, axial[v, k], am)
        high, low = split(am)
        adj[v] = jnp.concatenate([high, high, low], axis=1)

    def build(v, carry):
        col = lax.broadcasted_iota(jnp.int32, (1, W), 1)
        at = col % RW
        for s in range(PEERS):
            at = jnp.where(col // RW == s, at + order[v, s] * RW, at)
        for b in range(W // 64):
            d = lax.broadcasted_iota(jnp.int32, (64, W), 0) + (b * 64 + HY) - at
            q = jnp.zeros((64, W), F32)
            for i in range(TLAT):
                q = jnp.where(d == i, lat[v, 1, i], q)
            high, low = split(q)
            qh[v, b * 64 : (b + 1) * 64, :] = high
            ql[v, b * 64 : (b + 1) * 64, :] = low
        return carry

    lax.fori_loop(0, NV, build, 0)

    for side in range(2):

        @pl.when(has_z[1 - side])
        def _():
            z_copy(side, 0).wait_recv()

        @pl.when(on_chip[1 - side])
        def _():
            z_copy(side, 1).wait_recv()
            z_copy(side, 2).wait_recv()

        for ys in range(2):

            @pl.when(across[1 - side] & has_y[1 - ys])
            def _():
                d_copy(side, ys).wait_recv()

    def axial_row(y, carry):
        high, low = split(ext[y])
        axb[y] = dot(acat[...], jnp.concatenate([high, low, high], axis=0))
        return carry

    lax.fori_loop(0, RE, axial_row, 0, unroll=4)

    def row_tile(t, carry):
        v = t // 2
        taps = [lat[v, 0, j] for j in range(TLAT)]
        at = pl.multiple_of(t * 16, 16)
        m = pl.multiple_of((t % 2) * 16, 16)
        for c in range(W // 128):
            cols = slice(c * 128, (c + 1) * 128)
            rows = [axb[y, pl.ds(at, 16), cols] for y in range(RE)]
            for y in range(RW):
                acc = taps[0] * rows[y]
                for j in range(1, TLAT):
                    acc = acc + taps[j] * rows[y + j]
                high, low = split(acc)
                lh[v, pl.ds(PLACE[y] * PL + m, 16), cols] = high
                ll[v, pl.ds(PLACE[y] * PL + m, 16), cols] = low
        return carry

    lax.fori_loop(0, NV * 2, row_tile, 0)

    def col_view(v, carry):
        for n in range(2):
            cols = slice(n * 256, (n + 1) * 256)
            res = dot(lh[v], qh[v, :, cols]) + dot(ll[v], qh[v, :, cols]) + dot(lh[v], ql[v, :, cols])
            bl[v, 2 * n] = res[:, :128]
            bl[v, 2 * n + 1] = res[:, 128:]
        return carry

    lax.fori_loop(0, NV, col_view, 0)

    def arrived(v):
        for h in range(len(parts_of(v, rcv, 0))):
            yield lambda h=h: pltpu.make_async_copy(
                parts_of(v, rcv, pl.ds(0, PEERS - 1))[h][0],
                parts_of(v, rcv, pl.ds(0, PEERS - 1))[h][0],
                a_recv.at[parts_of(v, rcv, 0)[h][1]],
            ).wait()

    def ratio(v, halves):
        def group(g, inner):
            for h in halves:
                for s in range(PEERS // 8):
                    cols = slice(s * 128, (s + 1) * 128)
                    vals = swap_chunks(
                        [rcv[v, s * 8 + k, g, h * 8 : (h + 1) * 8] for k in range(8)], RW
                    )
                    vals = [
                        vals[z] / bl[v, s, pl.ds(h * 256 + g * 8 + z, 8, stride=PL), :]
                        for z in range(8)
                    ]
                    for z in range(0, 8, 2):
                        high, low = split(jnp.concatenate(vals[z : z + 2], axis=0))
                        at = pl.multiple_of(h * 256 + g * 64 + z * 8, 16)
                        rh[pl.ds(at, 16), cols] = high
                        rl[pl.ds(at, 16), cols] = low
            return inner

        lax.fori_loop(0, ZG, group, 0)

    def columns_back(v, start, stop):
        at = slice(start, stop)
        for n in range(2):
            rows = slice(n * 256, (n + 1) * 256)
            res = (
                dot_nt(rh[at], qh[v, rows, :]) + dot_nt(rl[at], qh[v, rows, :]) + dot_nt(rh[at], ql[v, rows, :])
            )
            bl[v, 2 * n, at] = res[:, :128]
            bl[v, 2 * n + 1, at] = res[:, 128:]

    def rows_back(v, outs):
        taps = [lat[v, 0, j] for j in range(TLAT)]
        used = sorted({y - j for y in outs for j in range(TLAT) if 0 <= y - j < RW})

        def spread(h, inner):
            for c in range(W // 128):
                cols = slice(c * 128, (c + 1) * 128)
                rows = {
                    y: bl[v, c, pl.ds(PLACE[y] // 8 * 256 + h * 128 + PLACE[y] % 8, 16, stride=8), :]
                    for y in used
                }
                for y in outs:
                    acc = None
                    for j in range(TLAT):
                        if 0 <= y - j < RW:
                            term = taps[j] * rows[y - j]
                            acc = term if acc is None else acc + term
                    high, low = split(acc)
                    at = pl.multiple_of(h * 16, 16)
                    tt[y, pl.ds(at, 16), cols] = high
                    tt[y, pl.ds(PL + at, 16), cols] = low
                    tt[y, pl.ds(2 * PL + at, 16), cols] = high
            return inner

        lax.fori_loop(0, 2, spread, 0)

    def axial_back(v, first, start, stop):
        def row(y, carry):
            term = dot(adj[v], tt[y])
            gb[y] = term if first else gb[y] + term
            return carry

        lax.fori_loop(start, stop, row, 0, unroll=4)

    def whole_view(v, first):
        for wait in arrived(v):
            wait()
        ratio(v, (0, 1))
        columns_back(v, 0, 512)
        rows_back(v, range(RE))
        axial_back(v, first, 0, RE)

    def next_view(v, carry):
        whole_view(v, False)
        return carry

    whole_view(0, True)
    lax.fori_loop(1, NV - 1, next_view, 0)

    last = NV - 1
    edge_in, inner_in = arrived(last)
    edge_in()
    ratio(last, (0,))
    columns_back(last, 0, 256)
    rows_back(last, EDGE)

    parts = ((0, HY), (HY + RW, RE), (HY, HY + RW))

    def zb_copy(side, part):
        src = (slice(0, HZ), slice(HZ + PL, PE))[side]
        rows = slice(*parts[part])
        return pltpu.make_async_remote_copy(
            gb.at[rows, src], zr.at[side, rows], zb_send.at[side, part], zb_recv.at[side, part],
            device_id=(gy, (dn_z, up_z)[side]), device_id_type=MESH,
        )

    def db_copy(zs, ys):
        rows = (slice(0, HY), slice(HY + RW, RE))[ys]
        src = (slice(0, HZ), slice(HZ + PL, PE))[zs]
        return pltpu.make_async_remote_copy(
            gb.at[rows, src], dr.at[zs, ys], db_send.at[zs, ys], db_recv.at[zs, ys],
            device_id=((dn_y, up_y)[ys], (dn_z, up_z)[zs]), device_id_type=MESH,
        )

    def zb_start(part):
        for side in range(2):

            @pl.when((has_z if part == 2 else on_chip)[side])
            def _():
                zb_copy(side, part).start()

    def zb_add(part):
        for side in range(2):

            @pl.when((has_z if part == 2 else on_chip)[1 - side])
            def _():
                zb_copy(side, part).wait_recv()
                at = (slice(PL, PL + HZ), slice(HZ, 2 * HZ))[side]
                for y in range(*parts[part]):
                    gb[y, at] = gb[y, at] + zr[side, y]

    for part in range(2):
        axial_back(last, False, *parts[part])
        zb_start(part)
    for zs in range(2):
        for ys in range(2):

            @pl.when(across[zs] & has_y[ys])
            def _():
                db_copy(zs, ys).start()

    for part in range(2):
        zb_add(part)

    def yb_copy(side):
        src = (slice(0, HY), slice(HY + RW, RE))[side]
        return pltpu.make_async_remote_copy(
            gb.at[src, HZ : HZ + PL], yr.at[side], yb_send.at[side], yb_recv.at[side],
            device_id=((dn_y, up_y)[side], gz), device_id_type=MESH,
        )

    for side in range(2):

        @pl.when(has_y[side])
        def _():
            yb_copy(side).start()

    inner_in()
    ratio(last, (1,))
    columns_back(last, 256, 512)
    rows_back(last, INNER)
    axial_back(last, False, *parts[2])
    zb_start(2)
    zb_add(2)

    def finish(rows):
        for c in range(CC):
            cols = slice(c * 128, (c + 1) * 128)
            for y in rows:
                est_v[c, pl.ds(y, PL, stride=RW), :] = ext[HY + y, HZ : HZ + PL, cols] * (
                    gb[HY + y, HZ : HZ + PL, cols] * (1.0 / NV)
                )

    finish(range(HY, RW - HY))
    for side in range(2):

        @pl.when(has_y[1 - side])
        def _():
            yb_copy(side).wait_recv()
            base = (RW, HY)[side]
            for y in range(HY):
                gb[base + y, HZ : HZ + PL] = gb[base + y, HZ : HZ + PL] + yr[side, y]

        for zs in range(2):

            @pl.when(across[1 - zs] & has_y[1 - side])
            def _():
                db_copy(zs, side).wait_recv()
                base = (RW, HY)[side]
                at = (slice(PL, PL + HZ), slice(HZ, 2 * HZ))[zs]
                for y in range(HY):
                    gb[base + y, at] = gb[base + y, at] + dr[zs, side, y]

    finish([*range(HY), *range(RW - HY, RW)])
    outs = []
    for c in range(CC):
        cols = slice(c * 128, (c + 1) * 128)
        outs.append(pltpu.make_async_copy(est_v.at[c], out_ref.at[:, cols], lsem.at[NV + c]))
        outs[-1].start()
    for copy in outs:
        copy.wait()

    for side in range(2):

        @pl.when(has_y[side])
        def _():
            y_copy(side).wait_send()
            yb_copy(side).wait_send()

        @pl.when(has_z[side])
        def _():
            z_copy(side, 0).wait_send()
            zb_copy(side, 2).wait_send()

        @pl.when(on_chip[side])
        def _():
            for part in range(2):
                z_copy(side, 1 + part).wait_send()
                zb_copy(side, part).wait_send()

        for ys in range(2):

            @pl.when(across[side] & has_y[ys])
            def _():
                d_copy(side, ys).wait_send()
                db_copy(side, ys).wait_send()

    for v in range(NV):
        for block, n in parts_of(v, snd, pl.ds(0, PEERS - 1)):
            pltpu.make_async_copy(block, block, a_send.at[n]).wait()


def local(estimate, observed, tile_order, lateral_taps, axial_taps):
    rows = PL * RW
    smem = pl.BlockSpec(memory_space=pltpu.SMEM)
    hbm = pl.BlockSpec(memory_space=pl.ANY)
    dma = pltpu.SemaphoreType.DMA
    out = pl.pallas_call(
        kernel,
        out_shape=jax.ShapeDtypeStruct((rows, W), F32),
        in_specs=[hbm, hbm, smem, smem, smem],
        out_specs=hbm,
        scratch_shapes=[
            pltpu.VMEM((CC, rows, 128), F32),
            pltpu.VMEM((NV, rows, W), F32),
            pltpu.VMEM((NV, PEERS, ZG, RW, 128), F32),
            pltpu.VMEM((NV, PEERS, ZG, RW, 128), F32),
            pltpu.VMEM((RE, PE, W), F32),
            pltpu.VMEM((RE, NV * PL, W), F32),
            pltpu.VMEM((NV, rows, W), BF16),
            pltpu.VMEM((NV, rows, W), BF16),
            pltpu.VMEM((NV, CC, rows, 128), F32),
            pltpu.VMEM((NV, W, W), BF16),
            pltpu.VMEM((NV, W, W), BF16),
            pltpu.VMEM((rows, W), BF16),
            pltpu.VMEM((rows, W), BF16),
            pltpu.VMEM((RE, 3 * PL, W), BF16),
            pltpu.VMEM((NV * PL, 3 * PE), BF16),
            pltpu.VMEM((NV, PE, 3 * PL), BF16),
            pltpu.VMEM((RE, PE, W), F32),
            pltpu.VMEM((2, RE, HZ, W), F32),
            pltpu.VMEM((2, HY, PL, W), F32),
            pltpu.VMEM((2, 2, HY, HZ, W), F32),
            dma((NV + CC,)),
            dma((NV + 1,)),
            dma((NV + 1,)),
            dma((2,)),
            dma((2,)),
            dma((2, 3)),
            dma((2, 3)),
            dma((2, 3)),
            dma((2, 3)),
            dma((2,)),
            dma((2,)),
            dma((2, 2)),
            dma((2, 2)),
            dma((2, 2)),
            dma((2, 2)),
        ],
        compiler_params=pltpu.CompilerParams(
            collective_id=0, has_side_effects=True, vmem_limit_bytes=60 << 20
        ),
    )(
        estimate.reshape(rows, W),
        observed.reshape(NV, rows, W),
        tile_order,
        lateral_taps,
        axial_taps,
    )
    return out.reshape(PL, RW, W)


def solution(mesh):
    return jax.shard_map(
        local,
        mesh=mesh,
        in_specs=(P("gz", "gy", None), P(None, "gz", "gy", None), P(), P(), P()),
        out_specs=P("gz", "gy", None),
        check_vma=False,
    )
```

```python
import functools

import jax
import jax.numpy as jnp
from jax import lax
from jax.experimental import pallas as pl
from jax.experimental.pallas import tpu as pltpu
from jax.sharding import PartitionSpec as P

MESH = pl.DeviceIdType.MESH
F32 = jnp.float32
BF16 = jnp.bfloat16

NV = 4
TAX = 33
TLAT = 9
PL = 32
RW = 16
W = 512
PEERS = 32
SLABS = 4
HZ = TAX // 2
HY = TLAT // 2
PE = PL + 2 * HZ
RE = RW + 2 * HY
ZG = PL // 8
CC = W // 128


PLANE = (
    (1, 0), (0, 1), (3, 0), (0, 3), (2, 1), (1, 2), (2, 3), (3, 2), (1, 1), (3, 3), (1, 3), (3, 1), (2, 0), (0, 2), (2, 2),
)
ORDER = tuple(
    sorted(
        ((0, 0, 1),) + tuple((dz, dy, dx) for dz, dy in PLANE for dx in (1, 0)),
        key=lambda o: -(min(o[0], 4 - o[0]) + min(o[1], 4 - o[1]) + o[2]),
    )
)


KEPT = (0, 1, 2, 3, 12, 13, 14, 15, 8, 9, 10, 11, 4, 5, 6, 7)
PLACE = tuple(KEPT.index(y) for y in range(RW))
EDGE = (*range(HY), *range(HY + RW, RE))
INNER = tuple(range(HY, HY + RW))


def split(value):
    high = value.astype(BF16)
    return high, (value - high.astype(F32)).astype(BF16)


def dot(a, b):
    return jnp.dot(a, b, preferred_element_type=F32)


def dot_nt(a, b):
    return lax.dot_general(a, b, (((1,), (1,)), ((), ())), preferred_element_type=F32)


def swap_chunks(vals, chunk):
    span = vals[0].shape[-1]
    which = lax.broadcasted_iota(jnp.int32, vals[0].shape, vals[0].ndim - 1) // chunk
    for b in (4, 2, 1):
        low = (which & b) == 0
        new = list(vals)
        for k in range(8):
            if k & b:
                continue
            new[k] = jnp.where(low, vals[k], pltpu.roll(vals[k | b], b * chunk, 1))
            new[k | b] = jnp.where(low, pltpu.roll(vals[k], span - b * chunk, 1), vals[k | b])
        vals = new
    return vals


def kernel(
    est_hbm, obs_hbm, order, lat, axial, out_ref,
    est_v, obs_v, snd, rcv, ext, axb, lh, ll, bl, qh, ql, rh, rl, tt, acat, adj, gb, zr, yr, dr,
    lsem, a_send, a_recv, y_send, y_recv, z_send, z_recv, zb_send, zb_recv, yb_send, yb_recv,
    d_send, d_recv, db_send, db_recv,
):
    gy = lax.axis_index("gy")
    gz = lax.axis_index("gz")
    cz, cy, cx = gy // 8, (gy // 2) % 4, gy % 2

    est_in = [
        pltpu.make_async_copy(est_hbm.at[:, c * 128 : (c + 1) * 128], est_v.at[c], lsem.at[NV + c])
        for c in range(CC)
    ]
    for copy in est_in:
        copy.start()
    for v in range(NV):
        pltpu.make_async_copy(obs_hbm.at[v], obs_v.at[v], lsem.at[v]).start()

    way = 1 - 2 * (gz % 2)

    def peer(dz, dy, dx):
        return ((cz + 4 + way * dz) % 4) * 8 + ((cy + 4 + way * dy) % 4) * 2 + (cx + dx) % 2

    bar = pltpu.get_barrier_semaphore()

    for offset in ORDER:
        pl.semaphore_signal(bar, inc=1, device_id=(peer(*offset), gz), device_id_type=MESH)
    up_z, dn_z = (gz + 1) % SLABS, (gz + SLABS - 1) % SLABS
    up_y, dn_y = (gy + 1) % PEERS, (gy + PEERS - 1) % PEERS
    for other in (up_z, dn_z):
        pl.semaphore_signal(bar, inc=1, device_id=(gy, other), device_id_type=MESH)

    middle = gz * (SLABS - 1 - gz) // 2

    @pl.when(middle == 1)
    def _():
        for other in (up_y, dn_y):
            pl.semaphore_signal(
                bar, inc=1, device_id=(other, SLABS - 1 - gz), device_id_type=MESH
            )

    for c, copy in enumerate(est_in):
        copy.wait()
        for y in range(RW):
            ext[HY + y, HZ : HZ + PL, c * 128 : (c + 1) * 128] = est_v[c, pl.ds(y, PL, stride=RW), :]

    @pl.when(gy == 0)
    def _():
        ext[0:HY, HZ : HZ + PL, :] = jnp.zeros((HY, PL, W), F32)

    @pl.when(gy == PEERS - 1)
    def _():
        ext[HY + RW : RE, HZ : HZ + PL, :] = jnp.zeros((HY, PL, W), F32)

    @pl.when(gz == 0)
    def _():
        ext[:, 0:HZ, :] = jnp.zeros((RE, HZ, W), F32)

    @pl.when(gz == SLABS - 1)
    def _():
        ext[:, HZ + PL : PE, :] = jnp.zeros((RE, HZ, W), F32)

    for z_edge, planes in ((1, slice(HZ + PL, PE)), (2, slice(0, HZ))):
        for y_edge, rows in ((0, slice(0, HY)), (PEERS - 1, slice(HY + RW, RE))):

            @pl.when((gz == z_edge) & (gy == y_edge))
            def _():
                ext[rows, planes, :] = jnp.zeros((HY, HZ, W), F32)

    pl.semaphore_wait(bar, PEERS - 1 + 2 + 2 * middle)

    def y_copy(side):
        src = (slice(HY, 2 * HY), slice(RW, RW + HY))[side]
        dst = (slice(HY + RW, RE), slice(0, HY))[side]
        return pltpu.make_async_remote_copy(
            ext.at[src, HZ : HZ + PL], ext.at[dst, HZ : HZ + PL], y_send.at[side], y_recv.at[side],
            device_id=((dn_y, up_y)[side], gz), device_id_type=MESH,
        )

    def z_copy(side, part):
        rows = (slice(HY, HY + RW), slice(0, HY), slice(HY + RW, RE))[part]
        src = (slice(HZ, 2 * HZ), slice(PL, PL + HZ))[side]
        dst = (slice(HZ + PL, PE), slice(0, HZ))[side]
        return pltpu.make_async_remote_copy(
            ext.at[rows, src], ext.at[rows, dst], z_send.at[side, part], z_recv.at[side, part],
            device_id=(gy, (dn_z, up_z)[side]), device_id_type=MESH,
        )

    def d_copy(zs, ys):
        rows = (slice(HY, 2 * HY), slice(RW, RW + HY))[ys]
        to_rows = (slice(HY + RW, RE), slice(0, HY))[ys]
        src = (slice(HZ, 2 * HZ), slice(PL, PL + HZ))[zs]
        dst = (slice(HZ + PL, PE), slice(0, HZ))[zs]
        return pltpu.make_async_remote_copy(
            ext.at[rows, src], ext.at[to_rows, dst], d_send.at[zs, ys], d_recv.at[zs, ys],
            device_id=((dn_y, up_y)[ys], (dn_z, up_z)[zs]), device_id_type=MESH,
        )

    on_chip = (gz % 2 == 1, gz % 2 == 0)
    across = (gz == 2, gz == 1)
    has_y = (gy > 0, gy < PEERS - 1)
    has_z = (gz > 0, gz < SLABS - 1)
    def y_piece(side, p):
        src = (HY, RW)[side]
        dst = (HY + RW, 0)[side]
        at = slice(HZ + p * 8, HZ + p * 8 + 8)

        @pl.when(has_y[side])
        def _():
            pltpu.make_async_remote_copy(
                ext.at[src : src + HY, at], ext.at[dst : dst + HY, at], y_send.at[side], y_recv.at[side],
                device_id=((dn_y, up_y)[side], gz), device_id_type=MESH,
            ).start()

    def z_piece(side, p):
        rows = slice(HY + 4 * p, HY + 4 * p + 4)
        src = (slice(HZ, 2 * HZ), slice(PL, PL + HZ))[side]
        dst = (slice(HZ + PL, PE), slice(0, HZ))[side]

        @pl.when(has_z[side])
        def _():
            pltpu.make_async_remote_copy(
                ext.at[rows, src], ext.at[rows, dst], z_send.at[side, 0], z_recv.at[side, 0],
                device_id=(gy, (dn_z, up_z)[side]), device_id_type=MESH,
            ).start()

    def d_piece(zs, ys):
        @pl.when(across[zs] & has_y[ys])
        def _():
            d_copy(zs, ys).start()

    y_pieces = [functools.partial(y_piece, side, p) for p in range(4) for side in range(2)]
    z_pieces = [functools.partial(z_piece, side, p) for p in range(4) for side in range(2)]
    z_pieces += [functools.partial(d_piece, a, b) for a in range(2) for b in range(2)]

    def send_margins():
        for side in range(2):

            @pl.when(has_y[1 - side])
            def _():
                y_copy(side).wait_recv()

        for side in range(2):

            @pl.when(on_chip[side])
            def _():
                z_copy(side, 1).start()
                z_copy(side, 2).start()

    upper = lax.broadcasted_iota(jnp.int32, (8, 128), 0) < HY

    def parts_of(v, ref, at):
        if isinstance(v, int) and v == NV - 1:
            return [(ref.at[v, at, :, h * 8 : (h + 1) * 8], v + h) for h in range(2)]
        return [(ref.at[v, at], v)]

    def send_view(v, carry, between=()):
        between = list(between)
        pltpu.make_async_copy(obs_hbm.at[v], obs_v.at[v], lsem.at[v]).wait()
        for g in range(ZG):
            for c in range(4):
                t = obs_v[v, g * 128 : (g + 1) * 128, c * 128 : (c + 1) * 128].T
                for d in range(8):
                    first = t[d * RW : d * RW + 8, :]
                    second = t[d * RW + 8 : (d + 1) * RW, :]
                    snd[v, c * 8 + d, g, 0:8] = jnp.where(upper, first, second)
                    snd[v, c * 8 + d, g, 8:RW] = jnp.where(upper, second, first)
        rcv[v, gy] = snd[v, gy]

        for h in range(len(parts_of(v, snd, 0))):
            for offset in ORDER:
                if between:
                    between.pop(0)()
                to = peer(*offset)
                src, n = parts_of(v, snd, to)[h]
                dst, _ = parts_of(v, rcv, gy)[h]
                pltpu.make_async_remote_copy(
                    src, dst, a_send.at[n], a_recv.at[n], device_id=(to, gz), device_id_type=MESH
                ).start()
        return carry

    for piece in y_pieces[:4]:
        piece()
    send_view(0, 0, y_pieces[4:] + z_pieces)
    send_view(1, 0)
    send_margins()
    lax.fori_loop(2, NV - 1, send_view, 0)
    send_view(NV - 1, 0)

    i0 = lax.broadcasted_iota(jnp.int32, (PL, PE), 0)
    i1 = lax.broadcasted_iota(jnp.int32, (PL, PE), 1)
    for v in range(NV):
        am = jnp.zeros((PL, PE), F32)
        for k in range(TAX):
            am = jnp.where(i1 - i0 == k, axial[v, k], am)
        high, low = split(am)
        acat[v * PL : (v + 1) * PL, :] = jnp.concatenate([high, high, low], axis=1)
    j0 = lax.broadcasted_iota(jnp.int32, (PE, PL), 0)
    j1 = lax.broadcasted_iota(jnp.int32, (PE, PL), 1)
    for v in range(NV):
        am = jnp.zeros((PE, PL), F32)
        for k in range(TAX):
            am = jnp.where(j0 - j1 == k, axial[v, k], am)
        high, low = split(am)
        adj[v] = jnp.concatenate([high, high, low], axis=1)

    def build(v, carry):
        col = lax.broadcasted_iota(jnp.int32, (1, W), 1)
        at = col % RW
        for s in range(PEERS):
            at = jnp.where(col // RW == s, at + order[v, s] * RW, at)
        for b in range(W // 64):
            d = lax.broadcasted_iota(jnp.int32, (64, W), 0) + (b * 64 + HY) - at
            q = jnp.zeros((64, W), F32)
            for i in range(TLAT):
                q = jnp.where(d == i, lat[v, 1, i], q)
            high, low = split(q)
            qh[v, b * 64 : (b + 1) * 64, :] = high
            ql[v, b * 64 : (b + 1) * 64, :] = low
        return carry

    lax.fori_loop(0, NV, build, 0)

    for side in range(2):

        @pl.when(has_z[1 - side])
        def _():
            z_copy(side, 0).wait_recv()

        @pl.when(on_chip[1 - side])
        def _():
            z_copy(side, 1).wait_recv()
            z_copy(side, 2).wait_recv()

        for ys in range(2):

            @pl.when(across[1 - side] & has_y[1 - ys])
            def _():
                d_copy(side, ys).wait_recv()

    def axial_row(y, carry):
        high, low = split(ext[y])
        axb[y] = dot(acat[...], jnp.concatenate([high, low, high], axis=0))
        return carry

    lax.fori_loop(0, RE, axial_row, 0, unroll=4)

    def row_tile(t, carry):
        v = t // 2
        taps = [lat[v, 0, j] for j in range(TLAT)]
        at = pl.multiple_of(t * 16, 16)
        m = pl.multiple_of((t % 2) * 16, 16)
        for c in range(W // 128):
            cols = slice(c * 128, (c + 1) * 128)
            rows = [axb[y, pl.ds(at, 16), cols] for y in range(RE)]
            for y in range(RW):
                acc = taps[0] * rows[y]
                for j in range(1, TLAT):
                    acc = acc + taps[j] * rows[y + j]
                high, low = split(acc)
                lh[v, pl.ds(PLACE[y] * PL + m, 16), cols] = high
                ll[v, pl.ds(PLACE[y] * PL + m, 16), cols] = low
        return carry

    lax.fori_loop(0, NV * 2, row_tile, 0)

    def col_view(v, carry):
        for n in range(2):
            cols = slice(n * 256, (n + 1) * 256)
            res = dot(lh[v], qh[v, :, cols]) + dot(ll[v], qh[v, :, cols]) + dot(lh[v], ql[v, :, cols])
            bl[v, 2 * n] = res[:, :128]
            bl[v, 2 * n + 1] = res[:, 128:]
        return carry

    lax.fori_loop(0, NV, col_view, 0)

    def arrived(v):
        for h in range(len(parts_of(v, rcv, 0))):
            yield lambda h=h: pltpu.make_async_copy(
                parts_of(v, rcv, pl.ds(0, PEERS - 1))[h][0],
                parts_of(v, rcv, pl.ds(0, PEERS - 1))[h][0],
                a_recv.at[parts_of(v, rcv, 0)[h][1]],
            ).wait()

    def ratio(v, halves):
        def group(g, inner):
            for h in halves:
                for s in range(PEERS // 8):
                    cols = slice(s * 128, (s + 1) * 128)
                    vals = swap_chunks(
                        [rcv[v, s * 8 + k, g, h * 8 : (h + 1) * 8] for k in range(8)], RW
                    )
                    vals = [
                        vals[z] / bl[v, s, pl.ds(h * 256 + g * 8 + z, 8, stride=PL), :]
                        for z in range(8)
                    ]
                    for z in range(0, 8, 2):
                        high, low = split(jnp.concatenate(vals[z : z + 2], axis=0))
                        at = pl.multiple_of(h * 256 + g * 64 + z * 8, 16)
                        rh[pl.ds(at, 16), cols] = high
                        rl[pl.ds(at, 16), cols] = low
            return inner

        lax.fori_loop(0, ZG, group, 0)

    def columns_back(v, start, stop):
        at = slice(start, stop)
        for n in range(2):
            rows = slice(n * 256, (n + 1) * 256)
            res = (
                dot_nt(rh[at], qh[v, rows, :]) + dot_nt(rl[at], qh[v, rows, :]) + dot_nt(rh[at], ql[v, rows, :])
            )
            bl[v, 2 * n, at] = res[:, :128]
            bl[v, 2 * n + 1, at] = res[:, 128:]

    def rows_back(v, outs):
        taps = [lat[v, 0, j] for j in range(TLAT)]
        used = sorted({y - j for y in outs for j in range(TLAT) if 0 <= y - j < RW})

        def spread(h, inner):
            for c in range(W // 128):
                cols = slice(c * 128, (c + 1) * 128)
                rows = {
                    y: bl[v, c, pl.ds(PLACE[y] // 8 * 256 + h * 128 + PLACE[y] % 8, 16, stride=8), :]
                    for y in used
                }
                for y in outs:
                    acc = None
                    for j in range(TLAT):
                        if 0 <= y - j < RW:
                            term = taps[j] * rows[y - j]
                            acc = term if acc is None else acc + term
                    high, low = split(acc)
                    at = pl.multiple_of(h * 16, 16)
                    tt[y, pl.ds(at, 16), cols] = high
                    tt[y, pl.ds(PL + at, 16), cols] = low
                    tt[y, pl.ds(2 * PL + at, 16), cols] = high
            return inner

        lax.fori_loop(0, 2, spread, 0)

    def axial_back(v, first, start, stop):
        def row(y, carry):
            term = dot(adj[v], tt[y])
            gb[y] = term if first else gb[y] + term
            return carry

        lax.fori_loop(start, stop, row, 0, unroll=4)

    def whole_view(v, first):
        for wait in arrived(v):
            wait()
        ratio(v, (0, 1))
        columns_back(v, 0, 512)
        rows_back(v, range(RE))
        axial_back(v, first, 0, RE)

    def next_view(v, carry):
        whole_view(v, False)
        return carry

    whole_view(0, True)
    lax.fori_loop(1, NV - 1, next_view, 0)

    last = NV - 1
    edge_in, inner_in = arrived(last)
    edge_in()
    ratio(last, (0,))
    columns_back(last, 0, 256)
    rows_back(last, EDGE)

    parts = ((0, HY), (HY + RW, RE), (HY, HY + RW))

    def zb_copy(side, part):
        src = (slice(0, HZ), slice(HZ + PL, PE))[side]
        rows = slice(*parts[part])
        return pltpu.make_async_remote_copy(
            gb.at[rows, src], zr.at[side, rows], zb_send.at[side, part], zb_recv.at[side, part],
            device_id=(gy, (dn_z, up_z)[side]), device_id_type=MESH,
        )

    def db_copy(zs, ys):
        rows = (slice(0, HY), slice(HY + RW, RE))[ys]
        src = (slice(0, HZ), slice(HZ + PL, PE))[zs]
        return pltpu.make_async_remote_copy(
            gb.at[rows, src], dr.at[zs, ys], db_send.at[zs, ys], db_recv.at[zs, ys],
            device_id=((dn_y, up_y)[ys], (dn_z, up_z)[zs]), device_id_type=MESH,
        )

    def zb_start(part):
        for side in range(2):

            @pl.when((has_z if part == 2 else on_chip)[side])
            def _():
                zb_copy(side, part).start()

    def zb_add(part):
        for side in range(2):

            @pl.when((has_z if part == 2 else on_chip)[1 - side])
            def _():
                zb_copy(side, part).wait_recv()
                at = (slice(PL, PL + HZ), slice(HZ, 2 * HZ))[side]
                for y in range(*parts[part]):
                    gb[y, at] = gb[y, at] + zr[side, y]

    for part in range(2):
        axial_back(last, False, *parts[part])
        zb_start(part)
    for zs in range(2):
        for ys in range(2):

            @pl.when(across[zs] & has_y[ys])
            def _():
                db_copy(zs, ys).start()

    for part in range(2):
        zb_add(part)

    def yb_copy(side):
        src = (slice(0, HY), slice(HY + RW, RE))[side]
        return pltpu.make_async_remote_copy(
            gb.at[src, HZ : HZ + PL], yr.at[side], yb_send.at[side], yb_recv.at[side],
            device_id=((dn_y, up_y)[side], gz), device_id_type=MESH,
        )

    for side in range(2):

        @pl.when(has_y[side])
        def _():
            yb_copy(side).start()

    inner_in()
    ratio(last, (1,))
    columns_back(last, 256, 512)
    rows_back(last, INNER)
    axial_back(last, False, *parts[2])
    zb_start(2)
    zb_add(2)

    def finish(rows):
        for c in range(CC):
            cols = slice(c * 128, (c + 1) * 128)
            for y in rows:
                est_v[c, pl.ds(y, PL, stride=RW), :] = ext[HY + y, HZ : HZ + PL, cols] * (
                    gb[HY + y, HZ : HZ + PL, cols] * (1.0 / NV)
                )

    finish(range(HY, RW - HY))
    for side in range(2):

        @pl.when(has_y[1 - side])
        def _():
            yb_copy(side).wait_recv()
            base = (RW, HY)[side]
            for y in range(HY):
                gb[base + y, HZ : HZ + PL] = gb[base + y, HZ : HZ + PL] + yr[side, y]

        for zs in range(2):

            @pl.when(across[1 - zs] & has_y[1 - side])
            def _():
                db_copy(zs, side).wait_recv()
                base = (RW, HY)[side]
                at = (slice(PL, PL + HZ), slice(HZ, 2 * HZ))[zs]
                for y in range(HY):
                    gb[base + y, at] = gb[base + y, at] + dr[zs, side, y]

    finish([*range(HY), *range(RW - HY, RW)])
    outs = []
    for c in range(CC):
        cols = slice(c * 128, (c + 1) * 128)
        outs.append(pltpu.make_async_copy(est_v.at[c], out_ref.at[:, cols], lsem.at[NV + c]))
        outs[-1].start()
    for copy in outs:
        copy.wait()

    for side in range(2):

        @pl.when(has_y[side])
        def _():
            y_copy(side).wait_send()
            yb_copy(side).wait_send()

        @pl.when(has_z[side])
        def _():
            z_copy(side, 0).wait_send()
            zb_copy(side, 2).wait_send()

        @pl.when(on_chip[side])
        def _():
            for part in range(2):
                z_copy(side, 1 + part).wait_send()
                zb_copy(side, part).wait_send()

        for ys in range(2):

            @pl.when(across[side] & has_y[ys])
            def _():
                d_copy(side, ys).wait_send()
                db_copy(side, ys).wait_send()

    for v in range(NV):
        for block, n in parts_of(v, snd, pl.ds(0, PEERS - 1)):
            pltpu.make_async_copy(block, block, a_send.at[n]).wait()


def local(estimate, observed, tile_order, lateral_taps, axial_taps):
    rows = PL * RW
    smem = pl.BlockSpec(memory_space=pltpu.SMEM)
    hbm = pl.BlockSpec(memory_space=pl.ANY)
    dma = pltpu.SemaphoreType.DMA
    out = pl.pallas_call(
        kernel,
        out_shape=jax.ShapeDtypeStruct((rows, W), F32),
        in_specs=[hbm, hbm, smem, smem, smem],
        out_specs=hbm,
        scratch_shapes=[
            pltpu.VMEM((CC, rows, 128), F32),
            pltpu.VMEM((NV, rows, W), F32),
            pltpu.VMEM((NV, PEERS, ZG, RW, 128), F32),
            pltpu.VMEM((NV, PEERS, ZG, RW, 128), F32),
            pltpu.VMEM((RE, PE, W), F32),
            pltpu.VMEM((RE, NV * PL, W), F32),
            pltpu.VMEM((NV, rows, W), BF16),
            pltpu.VMEM((NV, rows, W), BF16),
            pltpu.VMEM((NV, CC, rows, 128), F32),
            pltpu.VMEM((NV, W, W), BF16),
            pltpu.VMEM((NV, W, W), BF16),
            pltpu.VMEM((rows, W), BF16),
            pltpu.VMEM((rows, W), BF16),
            pltpu.VMEM((RE, 3 * PL, W), BF16),
            pltpu.VMEM((NV * PL, 3 * PE), BF16),
            pltpu.VMEM((NV, PE, 3 * PL), BF16),
            pltpu.VMEM((RE, PE, W), F32),
            pltpu.VMEM((2, RE, HZ, W), F32),
            pltpu.VMEM((2, HY, PL, W), F32),
            pltpu.VMEM((2, 2, HY, HZ, W), F32),
            dma((NV + CC,)),
            dma((NV + 1,)),
            dma((NV + 1,)),
            dma((2,)),
            dma((2,)),
            dma((2, 3)),
            dma((2, 3)),
            dma((2, 3)),
            dma((2, 3)),
            dma((2,)),
            dma((2,)),
            dma((2, 2)),
            dma((2, 2)),
            dma((2, 2)),
            dma((2, 2)),
        ],
        compiler_params=pltpu.CompilerParams(
            collective_id=0, has_side_effects=True, vmem_limit_bytes=60 << 20
        ),
    )(
        estimate.reshape(rows, W),
        observed.reshape(NV, rows, W),
        tile_order,
        lateral_taps,
        axial_taps,
    )
    return out.reshape(PL, RW, W)


def solution(mesh):
    return jax.shard_map(
        local,
        mesh=mesh,
        in_specs=(P("gz", "gy", None), P(None, "gz", "gy", None), P(), P(), P()),
        out_specs=P("gz", "gy", None),
        check_vma=False,
    )
```

```python
import functools

import jax
import jax.numpy as jnp
from jax import lax
from jax.experimental import pallas as pl
from jax.experimental.pallas import tpu as pltpu
from jax.sharding import PartitionSpec as P

MESH = pl.DeviceIdType.MESH
F32 = jnp.float32
BF16 = jnp.bfloat16

NV = 4
TAX = 33
TLAT = 9
PL = 32
RW = 16
W = 512
PEERS = 32
SLABS = 4
HZ = TAX // 2
HY = TLAT // 2
PE = PL + 2 * HZ
RE = RW + 2 * HY
ZG = PL // 8
CC = W // 128


PLANE = (
    (1, 0), (0, 1), (3, 0), (0, 3), (2, 1), (1, 2), (2, 3), (3, 2), (1, 1), (3, 3), (1, 3), (3, 1), (2, 0), (0, 2), (2, 2),
)
ORDER = tuple(
    sorted(
        ((0, 0, 1),) + tuple((dz, dy, dx) for dz, dy in PLANE for dx in (1, 0)),
        key=lambda o: -(min(o[0], 4 - o[0]) + min(o[1], 4 - o[1]) + o[2]),
    )
)


KEPT = (0, 1, 2, 3, 12, 13, 14, 15, 8, 9, 10, 11, 4, 5, 6, 7)
PLACE = tuple(KEPT.index(y) for y in range(RW))
EDGE = (*range(HY), *range(HY + RW, RE))
INNER = tuple(range(HY, HY + RW))


def split(value):
    high = value.astype(BF16)
    return high, (value - high.astype(F32)).astype(BF16)


def dot(a, b):
    return jnp.dot(a, b, preferred_element_type=F32)


def dot_nt(a, b):
    return lax.dot_general(a, b, (((1,), (1,)), ((), ())), preferred_element_type=F32)


def swap_chunks(vals, chunk):
    span = vals[0].shape[-1]
    which = lax.broadcasted_iota(jnp.int32, vals[0].shape, vals[0].ndim - 1) // chunk
    for b in (4, 2, 1):
        low = (which & b) == 0
        new = list(vals)
        for k in range(8):
            if k & b:
                continue
            new[k] = jnp.where(low, vals[k], pltpu.roll(vals[k | b], b * chunk, 1))
            new[k | b] = jnp.where(low, pltpu.roll(vals[k], span - b * chunk, 1), vals[k | b])
        vals = new
    return vals


def kernel(
    est_hbm, obs_hbm, order, lat, axial, out_ref,
    est_v, obs_v, snd, rcv, ext, axb, lh, ll, bl, qh, ql, rh, rl, tt, acat, adj, gb, zr, yr, dr,
    lsem, a_send, a_recv, y_send, y_recv, z_send, z_recv, zb_send, zb_recv, yb_send, yb_recv,
    d_send, d_recv, db_send, db_recv,
):
    gy = lax.axis_index("gy")
    gz = lax.axis_index("gz")
    cz, cy, cx = gy // 8, (gy // 2) % 4, gy % 2

    est_in = [
        pltpu.make_async_copy(est_hbm.at[:, c * 128 : (c + 1) * 128], est_v.at[c], lsem.at[NV + c])
        for c in range(CC)
    ]
    for copy in est_in:
        copy.start()
    for v in range(NV):
        pltpu.make_async_copy(obs_hbm.at[v], obs_v.at[v], lsem.at[v]).start()

    def peer(dz, dy, dx):
        return ((cz + dz) % 4) * 8 + ((cy + dy) % 4) * 2 + (cx + dx) % 2

    bar = pltpu.get_barrier_semaphore()

    for offset in ORDER:
        pl.semaphore_signal(bar, inc=1, device_id=(peer(*offset), gz), device_id_type=MESH)
    up_z, dn_z = (gz + 1) % SLABS, (gz + SLABS - 1) % SLABS
    up_y, dn_y = (gy + 1) % PEERS, (gy + PEERS - 1) % PEERS
    for other in (up_z, dn_z):
        pl.semaphore_signal(bar, inc=1, device_id=(gy, other), device_id_type=MESH)

    middle = gz * (SLABS - 1 - gz) // 2

    @pl.when(middle == 1)
    def _():
        for other in (up_y, dn_y):
            pl.semaphore_signal(
                bar, inc=1, device_id=(other, SLABS - 1 - gz), device_id_type=MESH
            )

    for c, copy in enumerate(est_in):
        copy.wait()
        for y in range(RW):
            ext[HY + y, HZ : HZ + PL, c * 128 : (c + 1) * 128] = est_v[c, pl.ds(y, PL, stride=RW), :]

    @pl.when(gy == 0)
    def _():
        ext[0:HY, HZ : HZ + PL, :] = jnp.zeros((HY, PL, W), F32)

    @pl.when(gy == PEERS - 1)
    def _():
        ext[HY + RW : RE, HZ : HZ + PL, :] = jnp.zeros((HY, PL, W), F32)

    @pl.when(gz == 0)
    def _():
        ext[:, 0:HZ, :] = jnp.zeros((RE, HZ, W), F32)

    @pl.when(gz == SLABS - 1)
    def _():
        ext[:, HZ + PL : PE, :] = jnp.zeros((RE, HZ, W), F32)

    for z_edge, planes in ((1, slice(HZ + PL, PE)), (2, slice(0, HZ))):
        for y_edge, rows in ((0, slice(0, HY)), (PEERS - 1, slice(HY + RW, RE))):

            @pl.when((gz == z_edge) & (gy == y_edge))
            def _():
                ext[rows, planes, :] = jnp.zeros((HY, HZ, W), F32)

    pl.semaphore_wait(bar, PEERS - 1 + 2 + 2 * middle)

    def y_copy(side):
        src = (slice(HY, 2 * HY), slice(RW, RW + HY))[side]
        dst = (slice(HY + RW, RE), slice(0, HY))[side]
        return pltpu.make_async_remote_copy(
            ext.at[src, HZ : HZ + PL], ext.at[dst, HZ : HZ + PL], y_send.at[side], y_recv.at[side],
            device_id=((dn_y, up_y)[side], gz), device_id_type=MESH,
        )

    def z_copy(side, part):
        rows = (slice(HY, HY + RW), slice(0, HY), slice(HY + RW, RE))[part]
        src = (slice(HZ, 2 * HZ), slice(PL, PL + HZ))[side]
        dst = (slice(HZ + PL, PE), slice(0, HZ))[side]
        return pltpu.make_async_remote_copy(
            ext.at[rows, src], ext.at[rows, dst], z_send.at[side, part], z_recv.at[side, part],
            device_id=(gy, (dn_z, up_z)[side]), device_id_type=MESH,
        )

    def d_copy(zs, ys):
        rows = (slice(HY, 2 * HY), slice(RW, RW + HY))[ys]
        to_rows = (slice(HY + RW, RE), slice(0, HY))[ys]
        src = (slice(HZ, 2 * HZ), slice(PL, PL + HZ))[zs]
        dst = (slice(HZ + PL, PE), slice(0, HZ))[zs]
        return pltpu.make_async_remote_copy(
            ext.at[rows, src], ext.at[to_rows, dst], d_send.at[zs, ys], d_recv.at[zs, ys],
            device_id=((dn_y, up_y)[ys], (dn_z, up_z)[zs]), device_id_type=MESH,
        )

    on_chip = (gz % 2 == 1, gz % 2 == 0)
    across = (gz == 2, gz == 1)
    has_y = (gy > 0, gy < PEERS - 1)
    has_z = (gz > 0, gz < SLABS - 1)
    def y_piece(side, p):
        src = (HY, RW)[side]
        dst = (HY + RW, 0)[side]
        at = slice(HZ + p * 8, HZ + p * 8 + 8)

        @pl.when(has_y[side])
        def _():
            pltpu.make_async_remote_copy(
                ext.at[src : src + HY, at], ext.at[dst : dst + HY, at], y_send.at[side], y_recv.at[side],
                device_id=((dn_y, up_y)[side], gz), device_id_type=MESH,
            ).start()

    def z_piece(side, p):
        rows = slice(HY + 4 * p, HY + 4 * p + 4)
        src = (slice(HZ, 2 * HZ), slice(PL, PL + HZ))[side]
        dst = (slice(HZ + PL, PE), slice(0, HZ))[side]

        @pl.when(has_z[side])
        def _():
            pltpu.make_async_remote_copy(
                ext.at[rows, src], ext.at[rows, dst], z_send.at[side, 0], z_recv.at[side, 0],
                device_id=(gy, (dn_z, up_z)[side]), device_id_type=MESH,
            ).start()

    def d_piece(zs, ys):
        @pl.when(across[zs] & has_y[ys])
        def _():
            d_copy(zs, ys).start()

    y_pieces = [functools.partial(y_piece, side, p) for p in range(4) for side in range(2)]
    z_pieces = [functools.partial(z_piece, side, p) for p in range(4) for side in range(2)]
    z_pieces += [functools.partial(d_piece, a, b) for a in range(2) for b in range(2)]

    def send_margins():
        for side in range(2):

            @pl.when(has_y[1 - side])
            def _():
                y_copy(side).wait_recv()

        for side in range(2):

            @pl.when(on_chip[side])
            def _():
                z_copy(side, 1).start()
                z_copy(side, 2).start()

    upper = lax.broadcasted_iota(jnp.int32, (8, 128), 0) < HY

    def parts_of(v, ref, at):
        if isinstance(v, int) and v == NV - 1:
            return [(ref.at[v, at, :, h * 8 : (h + 1) * 8], v + h) for h in range(2)]
        return [(ref.at[v, at], v)]

    def send_view(v, carry, between=()):
        between = list(between)
        pltpu.make_async_copy(obs_hbm.at[v], obs_v.at[v], lsem.at[v]).wait()
        for g in range(ZG):
            for c in range(4):
                t = obs_v[v, g * 128 : (g + 1) * 128, c * 128 : (c + 1) * 128].T
                for d in range(8):
                    first = t[d * RW : d * RW + 8, :]
                    second = t[d * RW + 8 : (d + 1) * RW, :]
                    snd[v, c * 8 + d, g, 0:8] = jnp.where(upper, first, second)
                    snd[v, c * 8 + d, g, 8:RW] = jnp.where(upper, second, first)
        rcv[v, gy] = snd[v, gy]

        for h in range(len(parts_of(v, snd, 0))):
            for offset in ORDER:
                if between:
                    between.pop(0)()
                to = peer(*offset)
                src, n = parts_of(v, snd, to)[h]
                dst, _ = parts_of(v, rcv, gy)[h]
                pltpu.make_async_remote_copy(
                    src, dst, a_send.at[n], a_recv.at[n], device_id=(to, gz), device_id_type=MESH
                ).start()
        return carry

    send_view(0, 0, y_pieces + z_pieces)
    send_view(1, 0)
    send_margins()
    lax.fori_loop(2, NV - 1, send_view, 0)
    send_view(NV - 1, 0)

    i0 = lax.broadcasted_iota(jnp.int32, (PL, PE), 0)
    i1 = lax.broadcasted_iota(jnp.int32, (PL, PE), 1)
    for v in range(NV):
        am = jnp.zeros((PL, PE), F32)
        for k in range(TAX):
            am = jnp.where(i1 - i0 == k, axial[v, k], am)
        high, low = split(am)
        acat[v * PL : (v + 1) * PL, :] = jnp.concatenate([high, high, low], axis=1)
    j0 = lax.broadcasted_iota(jnp.int32, (PE, PL), 0)
    j1 = lax.broadcasted_iota(jnp.int32, (PE, PL), 1)
    for v in range(NV):
        am = jnp.zeros((PE, PL), F32)
        for k in range(TAX):
            am = jnp.where(j0 - j1 == k, axial[v, k], am)
        high, low = split(am)
        adj[v] = jnp.concatenate([high, high, low], axis=1)

    def build(v, carry):
        col = lax.broadcasted_iota(jnp.int32, (1, W), 1)
        at = col % RW
        for s in range(PEERS):
            at = jnp.where(col // RW == s, at + order[v, s] * RW, at)
        for b in range(W // 64):
            d = lax.broadcasted_iota(jnp.int32, (64, W), 0) + (b * 64 + HY) - at
            q = jnp.zeros((64, W), F32)
            for i in range(TLAT):
                q = jnp.where(d == i, lat[v, 1, i], q)
            high, low = split(q)
            qh[v, b * 64 : (b + 1) * 64, :] = high
            ql[v, b * 64 : (b + 1) * 64, :] = low
        return carry

    lax.fori_loop(0, NV, build, 0)

    for side in range(2):

        @pl.when(has_z[1 - side])
        def _():
            z_copy(side, 0).wait_recv()

        @pl.when(on_chip[1 - side])
        def _():
            z_copy(side, 1).wait_recv()
            z_copy(side, 2).wait_recv()

        for ys in range(2):

            @pl.when(across[1 - side] & has_y[1 - ys])
            def _():
                d_copy(side, ys).wait_recv()

    def axial_row(y, carry):
        high, low = split(ext[y])
        axb[y] = dot(acat[...], jnp.concatenate([high, low, high], axis=0))
        return carry

    lax.fori_loop(0, RE, axial_row, 0, unroll=4)

    def row_tile(t, carry):
        v = t // 2
        taps = [lat[v, 0, j] for j in range(TLAT)]
        at = pl.multiple_of(t * 16, 16)
        m = pl.multiple_of((t % 2) * 16, 16)
        for c in range(W // 128):
            cols = slice(c * 128, (c + 1) * 128)
            rows = [axb[y, pl.ds(at, 16), cols] for y in range(RE)]
            for y in range(RW):
                acc = taps[0] * rows[y]
                for j in range(1, TLAT):
                    acc = acc + taps[j] * rows[y + j]
                high, low = split(acc)
                lh[v, pl.ds(PLACE[y] * PL + m, 16), cols] = high
                ll[v, pl.ds(PLACE[y] * PL + m, 16), cols] = low
        return carry

    lax.fori_loop(0, NV * 2, row_tile, 0)

    def col_view(v, carry):
        for n in range(2):
            cols = slice(n * 256, (n + 1) * 256)
            res = dot(lh[v], qh[v, :, cols]) + dot(ll[v], qh[v, :, cols]) + dot(lh[v], ql[v, :, cols])
            bl[v, 2 * n] = res[:, :128]
            bl[v, 2 * n + 1] = res[:, 128:]
        return carry

    lax.fori_loop(0, NV, col_view, 0)

    def arrived(v):
        for h in range(len(parts_of(v, rcv, 0))):
            yield lambda h=h: pltpu.make_async_copy(
                parts_of(v, rcv, pl.ds(0, PEERS - 1))[h][0],
                parts_of(v, rcv, pl.ds(0, PEERS - 1))[h][0],
                a_recv.at[parts_of(v, rcv, 0)[h][1]],
            ).wait()

    def ratio(v, halves):
        def group(g, inner):
            for h in halves:
                for s in range(PEERS // 8):
                    cols = slice(s * 128, (s + 1) * 128)
                    vals = swap_chunks(
                        [rcv[v, s * 8 + k, g, h * 8 : (h + 1) * 8] for k in range(8)], RW
                    )
                    vals = [
                        vals[z] / bl[v, s, pl.ds(h * 256 + g * 8 + z, 8, stride=PL), :]
                        for z in range(8)
                    ]
                    for z in range(0, 8, 2):
                        high, low = split(jnp.concatenate(vals[z : z + 2], axis=0))
                        at = pl.multiple_of(h * 256 + g * 64 + z * 8, 16)
                        rh[pl.ds(at, 16), cols] = high
                        rl[pl.ds(at, 16), cols] = low
            return inner

        lax.fori_loop(0, ZG, group, 0)

    def columns_back(v, start, stop):
        at = slice(start, stop)
        for n in range(2):
            rows = slice(n * 256, (n + 1) * 256)
            res = (
                dot_nt(rh[at], qh[v, rows, :]) + dot_nt(rl[at], qh[v, rows, :]) + dot_nt(rh[at], ql[v, rows, :])
            )
            bl[v, 2 * n, at] = res[:, :128]
            bl[v, 2 * n + 1, at] = res[:, 128:]

    def rows_back(v, outs):
        taps = [lat[v, 0, j] for j in range(TLAT)]
        used = sorted({y - j for y in outs for j in range(TLAT) if 0 <= y - j < RW})

        def spread(h, inner):
            for c in range(W // 128):
                cols = slice(c * 128, (c + 1) * 128)
                rows = {
                    y: bl[v, c, pl.ds(PLACE[y] // 8 * 256 + h * 128 + PLACE[y] % 8, 16, stride=8), :]
                    for y in used
                }
                for y in outs:
                    acc = None
                    for j in range(TLAT):
                        if 0 <= y - j < RW:
                            term = taps[j] * rows[y - j]
                            acc = term if acc is None else acc + term
                    high, low = split(acc)
                    at = pl.multiple_of(h * 16, 16)
                    tt[y, pl.ds(at, 16), cols] = high
                    tt[y, pl.ds(PL + at, 16), cols] = low
                    tt[y, pl.ds(2 * PL + at, 16), cols] = high
            return inner

        lax.fori_loop(0, 2, spread, 0)

    def axial_back(v, first, start, stop):
        def row(y, carry):
            term = dot(adj[v], tt[y])
            gb[y] = term if first else gb[y] + term
            return carry

        lax.fori_loop(start, stop, row, 0, unroll=4)

    def whole_view(v, first):
        for wait in arrived(v):
            wait()
        ratio(v, (0, 1))
        columns_back(v, 0, 512)
        rows_back(v, range(RE))
        axial_back(v, first, 0, RE)

    def next_view(v, carry):
        whole_view(v, False)
        return carry

    whole_view(0, True)
    lax.fori_loop(1, NV - 1, next_view, 0)

    last = NV - 1
    edge_in, inner_in = arrived(last)
    edge_in()
    ratio(last, (0,))
    columns_back(last, 0, 256)
    rows_back(last, EDGE)

    parts = ((0, HY), (HY + RW, RE), (HY, HY + RW))

    def zb_copy(side, part):
        src = (slice(0, HZ), slice(HZ + PL, PE))[side]
        rows = slice(*parts[part])
        return pltpu.make_async_remote_copy(
            gb.at[rows, src], zr.at[side, rows], zb_send.at[side, part], zb_recv.at[side, part],
            device_id=(gy, (dn_z, up_z)[side]), device_id_type=MESH,
        )

    def db_copy(zs, ys):
        rows = (slice(0, HY), slice(HY + RW, RE))[ys]
        src = (slice(0, HZ), slice(HZ + PL, PE))[zs]
        return pltpu.make_async_remote_copy(
            gb.at[rows, src], dr.at[zs, ys], db_send.at[zs, ys], db_recv.at[zs, ys],
            device_id=((dn_y, up_y)[ys], (dn_z, up_z)[zs]), device_id_type=MESH,
        )

    def zb_start(part):
        for side in range(2):

            @pl.when((has_z if part == 2 else on_chip)[side])
            def _():
                zb_copy(side, part).start()

    def zb_add(part):
        for side in range(2):

            @pl.when((has_z if part == 2 else on_chip)[1 - side])
            def _():
                zb_copy(side, part).wait_recv()
                at = (slice(PL, PL + HZ), slice(HZ, 2 * HZ))[side]
                for y in range(*parts[part]):
                    gb[y, at] = gb[y, at] + zr[side, y]

    for part in range(2):
        axial_back(last, False, *parts[part])
        zb_start(part)
    for zs in range(2):
        for ys in range(2):

            @pl.when(across[zs] & has_y[ys])
            def _():
                db_copy(zs, ys).start()

    for part in range(2):
        zb_add(part)

    def yb_copy(side):
        src = (slice(0, HY), slice(HY + RW, RE))[side]
        return pltpu.make_async_remote_copy(
            gb.at[src, HZ : HZ + PL], yr.at[side], yb_send.at[side], yb_recv.at[side],
            device_id=((dn_y, up_y)[side], gz), device_id_type=MESH,
        )

    for side in range(2):

        @pl.when(has_y[side])
        def _():
            yb_copy(side).start()

    inner_in()
    ratio(last, (1,))
    columns_back(last, 256, 512)
    rows_back(last, INNER)
    axial_back(last, False, *parts[2])
    zb_start(2)
    zb_add(2)

    def finish(rows, chunks=range(CC)):
        for c in chunks:
            cols = slice(c * 128, (c + 1) * 128)
            for y in rows:
                est_v[c, pl.ds(y, PL, stride=RW), :] = ext[HY + y, HZ : HZ + PL, cols] * (
                    gb[HY + y, HZ : HZ + PL, cols] * (1.0 / NV)
                )

    finish(range(HY, RW - HY))
    for side in range(2):

        @pl.when(has_y[1 - side])
        def _():
            yb_copy(side).wait_recv()
            base = (RW, HY)[side]
            for y in range(HY):
                gb[base + y, HZ : HZ + PL] = gb[base + y, HZ : HZ + PL] + yr[side, y]

        for zs in range(2):

            @pl.when(across[1 - zs] & has_y[1 - side])
            def _():
                db_copy(zs, side).wait_recv()
                base = (RW, HY)[side]
                at = (slice(PL, PL + HZ), slice(HZ, 2 * HZ))[zs]
                for y in range(HY):
                    gb[base + y, at] = gb[base + y, at] + dr[zs, side, y]

    outs = []
    for c in range(CC):
        finish([*range(HY), *range(RW - HY, RW)], [c])
        cols = slice(c * 128, (c + 1) * 128)
        outs.append(pltpu.make_async_copy(est_v.at[c], out_ref.at[:, cols], lsem.at[NV + c]))
        outs[-1].start()

    for side in range(2):

        @pl.when(has_y[side])
        def _():
            y_copy(side).wait_send()
            yb_copy(side).wait_send()

        @pl.when(has_z[side])
        def _():
            z_copy(side, 0).wait_send()
            zb_copy(side, 2).wait_send()

        @pl.when(on_chip[side])
        def _():
            for part in range(2):
                z_copy(side, 1 + part).wait_send()
                zb_copy(side, part).wait_send()

        for ys in range(2):

            @pl.when(across[side] & has_y[ys])
            def _():
                d_copy(side, ys).wait_send()
                db_copy(side, ys).wait_send()

    for v in range(NV):
        for block, n in parts_of(v, snd, pl.ds(0, PEERS - 1)):
            pltpu.make_async_copy(block, block, a_send.at[n]).wait()
    for copy in outs:
        copy.wait()


def local(estimate, observed, tile_order, lateral_taps, axial_taps):
    rows = PL * RW
    smem = pl.BlockSpec(memory_space=pltpu.SMEM)
    hbm = pl.BlockSpec(memory_space=pl.ANY)
    dma = pltpu.SemaphoreType.DMA
    out = pl.pallas_call(
        kernel,
        out_shape=jax.ShapeDtypeStruct((rows, W), F32),
        in_specs=[hbm, hbm, smem, smem, smem],
        out_specs=hbm,
        scratch_shapes=[
            pltpu.VMEM((CC, rows, 128), F32),
            pltpu.VMEM((NV, rows, W), F32),
            pltpu.VMEM((NV, PEERS, ZG, RW, 128), F32),
            pltpu.VMEM((NV, PEERS, ZG, RW, 128), F32),
            pltpu.VMEM((RE, PE, W), F32),
            pltpu.VMEM((RE, NV * PL, W), F32),
            pltpu.VMEM((NV, rows, W), BF16),
            pltpu.VMEM((NV, rows, W), BF16),
            pltpu.VMEM((NV, CC, rows, 128), F32),
            pltpu.VMEM((NV, W, W), BF16),
            pltpu.VMEM((NV, W, W), BF16),
            pltpu.VMEM((rows, W), BF16),
            pltpu.VMEM((rows, W), BF16),
            pltpu.VMEM((RE, 3 * PL, W), BF16),
            pltpu.VMEM((NV * PL, 3 * PE), BF16),
            pltpu.VMEM((NV, PE, 3 * PL), BF16),
            pltpu.VMEM((RE, PE, W), F32),
            pltpu.VMEM((2, RE, HZ, W), F32),
            pltpu.VMEM((2, HY, PL, W), F32),
            pltpu.VMEM((2, 2, HY, HZ, W), F32),
            dma((NV + CC,)),
            dma((NV + 1,)),
            dma((NV + 1,)),
            dma((2,)),
            dma((2,)),
            dma((2, 3)),
            dma((2, 3)),
            dma((2, 3)),
            dma((2, 3)),
            dma((2,)),
            dma((2,)),
            dma((2, 2)),
            dma((2, 2)),
            dma((2, 2)),
            dma((2, 2)),
        ],
        compiler_params=pltpu.CompilerParams(
            collective_id=0, has_side_effects=True, vmem_limit_bytes=60 << 20
        ),
    )(
        estimate.reshape(rows, W),
        observed.reshape(NV, rows, W),
        tile_order,
        lateral_taps,
        axial_taps,
    )
    return out.reshape(PL, RW, W)


def solution(mesh):
    return jax.shard_map(
        local,
        mesh=mesh,
        in_specs=(P("gz", "gy", None), P(None, "gz", "gy", None), P(), P(), P()),
        out_specs=P("gz", "gy", None),
        check_vma=False,
    )
```
